128 devices in a mesh: row: 8 (over z, core), col: 16 (over x, y).
Axes of the slice: x: 4, y: 4, z: 4, core: 2. Of those that a mesh axis runs over, the one named last changes fastest.
Arguments:
- point_values: bfloat16 [32, 1048576], P(None, ('row', 'col')), may hold values from -6 to 6
- point_coords: float32 [3, 1048576], P(None, ('row', 'col')), may hold values from 0 to 1
- leaf_order: int32 [1048576], P(('row', 'col')), may hold values from 0 to 8191, as said below
- leaf_bases: float32 [4096, 64, 256], P(('row', 'col')), may hold values from -0.375 to 0.375
- fine_transfer: float32 [8064, 64, 64], P(('row', 'col')), may hold values from -0.625 to 0.625
- coarse_transfer: float32 [126, 64, 64], replicated, may hold values from -0.625 to 0.625
- near_list: int32 [4096, 16], P(('row', 'col')), may hold values from 0 to 4095, as said below
- near_count: int32 [4096], P(('row', 'col')), may hold values from 1 to 16, as said below
- fine_far: int32 [8064, 16], P(('row', 'col')), may hold values from 0 to 4095, as said below
- fine_far_count: int32 [8064], P(('row', 'col')), may hold values from 1 to 16
- coarse_far: int32 [126, 16], replicated, may hold values from 0 to 63, as said below
- coarse_far_count: int32 [126], replicated, may hold values from 1 to 16
Outputs:
- product: float32 [32, 1048576], P(None, ('row', 'col'))
The draws below stay inside these ranges and needn't reach their ends.
Inputs may be any that keep to these rules, and one draw needn't show every extreme that they name: `leaf_order`: on each device the 8192 entries are a permutation of 0 to 8191. `near_list`: entry 0 of leaf n's list is n itself; its other live entries are distinct leaves of the same device or of the devices just before and after it in the order of devices (row+col); entries from near_count on repeat n. `near_count`: summed over one device's leaves the counts are at most 384; some device has exactly 384. `fine_far`: entries are nodes of the same level, by index in that level's order; live ones are distinct, never the node itself, and belong to the same device or to the devices just before and after it; entries from the count on repeat the first. `coarse_far`: entries are nodes of the same level, by index in that level; live ones are distinct and never the node itself; entries from the count on repeat the first.
All inputs are finite; a program needn't handle non-finite values.
Results may differ from the reference program's by a relative error of at most 0.0003.
Values sent between devices are 32-bit elements; how exact they have to be, the bound alone decides.
No kernel may reach another device: no remote copies, remote signals or barrier semaphores. Data moves between devices by JAX's collectives and lax.ppermute only.
A program may use at most 192 MiB of HBM per device.

```python
import math
import jax
import jax.numpy as jnp
from jax import lax

LEAF = 256
RANK = 64
NVEC = 32
LEAF_DEV = 32
NEAR_MAX = 16
FAR_MAX = 16
LEAVES = 4096
PTS_DEV = 8192
POINTS = 1048576
NODES_DEV = 63
N_ROW = 8
N_COL = 16
DEVICES = 128


def draw_leaf_order(key, part):
    key = jax.random.fold_in(key, 1)

    def shuffle_one(subkey):
        return jax.random.permutation(subkey, PTS_DEV)
    shuffled = jax.vmap(shuffle_one)(jax.random.split(key, DEVICES))
    return shuffled.reshape(-1).astype(jnp.int32)


def near_counts(key):
    key = jax.random.fold_in(key, 11)
    first_key, second_key, heavy_key, flip_key = jax.random.split(key, 4)
    pairs = LEAVES // 2
    lowest = max(1, NEAR_MAX // 4)
    first = jax.random.randint(first_key, (pairs,), lowest, NEAR_MAX + 1)
    second = jnp.minimum(jax.random.randint(second_key, (pairs,), lowest, NEAR_MAX + 1), 3 * NEAR_MAX // 2 - first)
    heavy = jax.random.randint(heavy_key, (), 0, DEVICES)
    on_heavy = jnp.arange(pairs) // (LEAF_DEV // 2) == heavy
    first = jnp.where(on_heavy, NEAR_MAX, first)
    second = jnp.where(on_heavy, NEAR_MAX // 2, second)
    flipped = jax.random.randint(flip_key, (pairs,), 0, 2) == 1
    left = jnp.where(flipped, second, first)
    right = jnp.where(flipped, first, second)
    return jnp.stack([left, right], axis=1).reshape(LEAVES).astype(jnp.int32)


def draw_near_count(key, part):
    return near_counts(key)


def draw_near_list(key, part):
    counts = near_counts(key)
    key = jax.random.fold_in(key, 12)
    leaves = jnp.arange(LEAVES, dtype=jnp.int32)
    window = 3 * LEAF_DEV
    candidates = (leaves // LEAF_DEV - 1)[:, None] * LEAF_DEV + jnp.arange(window, dtype=jnp.int32)[None, :]
    valid = (candidates >= 0) & (candidates < LEAVES) & (candidates != leaves[:, None])

    def shuffle_one(subkey):
        return jax.random.permutation(subkey, window)
    ranks = jax.vmap(shuffle_one)(jax.random.split(key, LEAVES)).astype(jnp.int32)
    score = (1 - valid.astype(jnp.int32)) * window + ranks
    picked = jnp.argsort(score, axis=1)[:, :NEAR_MAX - 1]
    chosen = jnp.take_along_axis(candidates, picked, axis=1)
    listed = jnp.concatenate([leaves[:, None], chosen], axis=1)
    slots = jnp.arange(NEAR_MAX)
    return jnp.where(slots[None, :] < counts[:, None], listed, leaves[:, None]).astype(jnp.int32)


def pick_lists(key, candidates, valid):
    rank_key, count_key, force_key = jax.random.split(key, 3)
    node_total, window = candidates.shape

    def shuffle_one(subkey):
        return jax.random.permutation(subkey, window)
    ranks = jax.vmap(shuffle_one)(jax.random.split(rank_key, node_total)).astype(jnp.int32)
    score = (1 - valid.astype(jnp.int32)) * window + ranks
    taken = min(window, FAR_MAX)
    picked = jnp.argsort(score, axis=1)[:, :taken]
    chosen = jnp.take_along_axis(candidates, picked, axis=1)
    if taken < FAR_MAX:
        chosen = jnp.concatenate([chosen, jnp.repeat(chosen[:, :1], FAR_MAX - taken, axis=1)], axis=1)
    available = jnp.sum(valid.astype(jnp.int32), axis=1)
    wanted = jax.random.randint(count_key, (node_total,), max(1, FAR_MAX // 4), FAR_MAX + 1)
    forced = jax.random.randint(force_key, (), 0, 8)
    wanted = jnp.where(jnp.arange(node_total) % 8 == forced, FAR_MAX, wanted)
    counts = jnp.minimum(wanted, available)
    slots = jnp.arange(FAR_MAX)
    lists = jnp.where(slots[None, :] < counts[:, None], chosen, chosen[:, :1])
    return (lists.astype(jnp.int32), counts.astype(jnp.int32))


def fine_lists(key):
    key = jax.random.fold_in(key, 21)
    lists, counts = ([], [])
    for height in range(LEAF_DEV.bit_length()):
        per_device = LEAF_DEV >> height
        node_total = DEVICES * per_device
        nodes = jnp.arange(node_total, dtype=jnp.int32)
        candidates = (nodes // per_device - 1)[:, None] * per_device + jnp.arange(3 * per_device, dtype=jnp.int32)[None, :]
        valid = (candidates >= 0) & (candidates < node_total) & (candidates != nodes[:, None])
        level_lists, level_counts = pick_lists(jax.random.fold_in(key, height), candidates, valid)
        lists.append(level_lists.reshape(DEVICES, per_device, FAR_MAX))
        counts.append(level_counts.reshape(DEVICES, per_device))
    return (jnp.concatenate(lists, axis=1).reshape(-1, FAR_MAX), jnp.concatenate(counts, axis=1).reshape(-1))


def coarse_lists(key):
    key = jax.random.fold_in(key, 31)
    lists, counts = ([], [])
    for height in range(1, DEVICES.bit_length() - 1):
        node_total = DEVICES >> height
        nodes = jnp.arange(node_total, dtype=jnp.int32)
        candidates = jnp.broadcast_to(nodes[None, :], (node_total, node_total))
        valid = candidates != nodes[:, None]
        level_lists, level_counts = pick_lists(jax.random.fold_in(key, height), candidates, valid)
        lists.append(level_lists)
        counts.append(level_counts)
    return (jnp.concatenate(lists, axis=0), jnp.concatenate(counts, axis=0))


def draw_fine_far(key, part):
    return fine_lists(key)[0]


def draw_fine_far_count(key, part):
    return fine_lists(key)[1]


def draw_coarse_far(key, part):
    return coarse_lists(key)[0]


def draw_coarse_far_count(key, part):
    return coarse_lists(key)[1]


def block_levels(stream_key, dims, cuts, low, top_value):
    def one(axis_at, blocks):
        draws = jax.random.uniform(jax.random.fold_in(jax.random.fold_in(stream_key, 6), axis_at), (blocks,), jnp.float32, low / len(cuts), top_value / len(cuts))
        return jnp.repeat(jnp.exp(draws), dims[axis_at] // blocks).reshape((-1,) + (1,) * (len(dims) - axis_at - 1))

    factor_of = one(*cuts[0])
    for cut in cuts[1:]:
        factor_of = factor_of * one(*cut)
    return factor_of


def centred(stream_key, shape, scale, limit, pieces=(), kind=jnp.bfloat16):
    values = scale * jax.random.normal(stream_key, shape, jnp.float32)
    if pieces:
        values = values * block_levels(stream_key, shape, pieces, -0.22, 0.18)
    return jnp.clip(values, -limit, limit).astype(kind)


def setup_inputs(seed: int = 0) -> dict:
    arg_keys = jax.random.split(jax.random.key(seed), 13)
    return {
        "point_values": centred(arg_keys[0], (NVEC, POINTS), 1.0, 6.0, ((1, 128),)),
        "point_coords": jnp.clip(1.0 * jax.random.uniform(arg_keys[1], (3, POINTS), jnp.float32) ** block_levels(arg_keys[1], (3, POINTS), ((1, 128),), -0.2, 0.2), 0.0, 1.0),
        "leaf_order": draw_leaf_order(jax.random.fold_in(arg_keys[12], 71), 0),
        "leaf_bases": centred(arg_keys[3], (LEAVES, RANK, LEAF), LEAF ** -0.5, 0.375, ((0, 128),), jnp.float32),
        "fine_transfer": centred(arg_keys[4], (N_ROW * N_COL * NODES_DEV, RANK, RANK), (3 * RANK // 2) ** -0.5, 0.625, ((0, 128),), jnp.float32),
        "coarse_transfer": centred(arg_keys[5], (N_ROW * N_COL - 2, RANK, RANK), (3 * RANK // 2) ** -0.5, 0.625, (), jnp.float32),
        "near_list": draw_near_list(jax.random.fold_in(arg_keys[12], 71), 0),
        "near_count": draw_near_count(jax.random.fold_in(arg_keys[12], 71), 0),
        "fine_far": draw_fine_far(jax.random.fold_in(arg_keys[12], 71), 0),
        "fine_far_count": draw_fine_far_count(jax.random.fold_in(arg_keys[12], 71), 0),
        "coarse_far": draw_coarse_far(jax.random.fold_in(arg_keys[12], 71), 0),
        "coarse_far_count": draw_coarse_far_count(jax.random.fold_in(arg_keys[12], 71), 0),
    }


length_scale = 0.2
highest = lax.Precision.HIGHEST

def matern(diff, axis):
    return jnp.exp(-jnp.sqrt(lax.optimization_barrier(jnp.sum(diff * diff, axis=axis))) / length_scale)

def skeletons(sorted_coords, node_total):
    stride = sorted_coords.shape[1] // (node_total * RANK)
    picked = sorted_coords.reshape(3, node_total, RANK, stride)[:, :, :, 0]
    return jnp.transpose(picked, (1, 0, 2))

def couple(coefs, skeleton, far_lists, far_counts):

    def one_node(inputs):
        entries, count, own = inputs
        source = skeleton[entries]
        block = matern(source[:, :, :, None] - own[None, :, None, :], 1)
        weight = (jnp.arange(FAR_MAX) < count).astype(jnp.float32)
        terms = coefs[entries] * weight[:, None, None]
        return jnp.einsum('svb,sba->va', terms, block, precision=highest) / math.sqrt(RANK)
    return lax.map(one_node, (far_lists, far_counts, skeleton))

def reference(point_values, point_coords, leaf_order, leaf_bases, fine_transfer, coarse_transfer, near_list, near_count, fine_far, fine_far_count, coarse_far, coarse_far_count):
    shift = jnp.arange(POINTS, dtype=jnp.int32) // PTS_DEV * PTS_DEV
    placed = (leaf_order + shift).astype(jnp.int32)
    sorted_values = point_values[:, placed]
    sorted_coords = point_coords[:, placed]
    values_leaf = sorted_values.reshape(NVEC, LEAVES, LEAF)
    coords_leaf = sorted_coords.reshape(3, LEAVES, LEAF)

    def near_leaf(inputs):
        target, sources, count = inputs
        diff = coords_leaf[:, sources][:, :, :, None] - coords_leaf[:, target][:, None, None, :]
        block = matern(diff, 0)
        terms = jnp.einsum('vsb,sba->sva', values_leaf[:, sources].astype(jnp.float32), block, precision=highest)
        weight = (jnp.arange(NEAR_MAX) < count).astype(jnp.float32)
        return lax.optimization_barrier(jnp.sum(terms * weight[:, None, None], axis=0))
    near = lax.map(near_leaf, (jnp.arange(LEAVES, dtype=jnp.int32), near_list, near_count))
    depth = LEAF_DEV.bit_length() - 1
    tops = DEVICES.bit_length() - 1
    sizes, transfers, far_lists, far_counts = ([], [], [], [])
    cursor = 0
    for height in range(depth + 1):
        per_device = LEAF_DEV >> height
        sizes.append(DEVICES * per_device)
        transfers.append(fine_transfer.reshape(DEVICES, NODES_DEV, RANK, RANK)[:, cursor:cursor + per_device].reshape(-1, RANK, RANK))
        far_lists.append(fine_far.reshape(DEVICES, NODES_DEV, FAR_MAX)[:, cursor:cursor + per_device].reshape(-1, FAR_MAX))
        far_counts.append(fine_far_count.reshape(DEVICES, NODES_DEV)[:, cursor:cursor + per_device].reshape(-1))
        cursor += per_device
    cursor = 0
    for height in range(1, tops):
        node_total = DEVICES >> height
        sizes.append(node_total)
        transfers.append(coarse_transfer[cursor:cursor + node_total])
        far_lists.append(coarse_far[cursor:cursor + node_total])
        far_counts.append(coarse_far_count[cursor:cursor + node_total])
        cursor += node_total
    sizes.append(1)
    coefs = [jnp.einsum('vnb,nrb->nvr', values_leaf.astype(jnp.float32), leaf_bases, precision=highest)]
    for index in range(len(sizes) - 1):
        lifted = jnp.einsum('nvr,nrs->nvs', coefs[index], transfers[index], precision=highest)
        coefs.append(lifted.reshape(sizes[index + 1], 2, NVEC, RANK).sum(axis=1))
    totals = jnp.zeros((1, NVEC, RANK), jnp.float32)
    for index in range(len(sizes) - 2, -1, -1):
        skeleton = skeletons(sorted_coords, sizes[index])
        coupled = couple(coefs[index], skeleton, far_lists[index], far_counts[index])
        totals = coupled + jnp.einsum('nvs,nrs->nvr', jnp.repeat(totals, 2, axis=0), transfers[index], precision=highest)
    far_field = jnp.einsum('nvr,nrb->vnb', totals, leaf_bases, precision=highest).reshape(NVEC, POINTS)
    near_field = jnp.transpose(near, (1, 0, 2)).reshape(NVEC, POINTS)
    result = near_field / math.sqrt(LEAF) + far_field
    return jnp.zeros((NVEC, POINTS), jnp.float32).at[:, placed].set(result)
```

```python
import functools

import jax
import jax.numpy as jnp
from jax import lax
from jax.experimental import pallas as pl
from jax.experimental.pallas import tpu as pltpu
from jax.sharding import PartitionSpec as P

exponent_scale = -1.4426950408889634 / 0.2
axes = ("row", "col")
f32, bf16 = jnp.float32, jnp.bfloat16
LEAVES, NODES, RANK, LEAF, NVEC, POINTS = 32, 63, 64, 256, 32, 8192
OFFSETS = (0, 32, 48, 56, 60, 62)
COARSE = (0, 0, 64, 96, 112, 120, 124)
UNROLL = 8
FAR_AWAY = 1e9
NT = (((1,), (1,)), ((), ()))
NN = (((1,), (0,)), ((), ()))
smem = pl.BlockSpec(memory_space=pltpu.SMEM)
vmem = pl.BlockSpec(memory_space=pltpu.VMEM)


def params(mib):
    return pltpu.CompilerParams(vmem_limit_bytes=mib << 20)


def split(x):
    hi = x.astype(bf16)
    return hi, (x - hi.astype(f32)).astype(bf16)


def dot(a, b, dims=NN):
    return lax.dot_general(a, b, dims, preferred_element_type=f32)


def dot3(a, b_hi, b_lo):
    m = a.shape[0]
    a_hi, a_lo = split(a)
    both = dot(jnp.concatenate([a_hi, a_lo], 0), b_hi)
    return both[:m] + both[m:] + dot(a_hi, b_lo)


def matern(cols, rows):
    d2 = None
    for col, row in zip(cols, rows):
        diff = col - row
        d2 = diff * diff if d2 is None else d2 + diff * diff
    return jnp.exp2(d2 * lax.rsqrt(jnp.maximum(d2, 1e-30)) * exponent_scale)


def column(row):
    return jnp.transpose(jnp.broadcast_to(row, (128, 128)))


def sort_kernel(
    pos_ref, order_ref, list_ref, count_ref, values_ref, coords_ref,
    packed_ref, skel_ref, top_ref, own_ref, other_ref, sizes_ref,
    rows, placed, picked, coarse,
):
    pos = pos_ref[0]

    def enter(block, carry):
        at = pl.multiple_of(block * 128, 128)
        tile = jnp.concatenate(
            [
                values_ref[:, pl.ds(at, 128)].astype(f32),
                coords_ref[:, pl.ds(at, 128)],
                jnp.zeros((5, 128), f32),
            ],
            0,
        )
        rows[pl.ds(at, 128), 0:40] = jnp.transpose(tile)
        return carry

    lax.fori_loop(0, POINTS // 128, enter, 0, unroll=4)

    def gather(step, carry):
        at = step * 32
        for u in range(32):
            placed[pl.ds(at + u, 1), :] = rows[pl.ds(order_ref[at + u], 1), :]
        return carry

    lax.fori_loop(0, POINTS // 32, gather, 0)

    for block in range(POINTS // 128):
        tile = jnp.transpose(placed[block * 128 : block * 128 + 128, :])
        group, lane = block // 8, (block % 8) * 128
        packed_ref[group * 32 : group * 32 + 32, lane : lane + 128] = tile[0:32]
        for c in range(3):
            at = 256 + c * 8 + group
            packed_ref[at : at + 1, lane : lane + 128] = tile[32 + c : 33 + c]

    pair = 0
    for height in range(6):
        total = LEAVES >> height
        stride = 4 << height
        for first in range(0, total, 2):
            if total == 1:
                for i in range(64):
                    picked[i : i + 1, :] = placed[i * stride : i * stride + 1, :]
                tile = jnp.transpose(picked[...])
            else:
                tile = jnp.transpose(placed[pl.ds(first * 64 * stride, 128, stride=stride), :])
            skel_ref[pair * 8 : pair * 8 + 8, :] = tile[32:40]
            pair += 1

    coarse[...] = jnp.zeros_like(coarse)
    for height in range(1, 7):
        share = 64 >> height
        start = (height - 1) * 64 + (pos & ((1 << height) - 1)) * share
        for i in range(share):
            coarse[pl.ds(start + i, 1), :] = placed[(i * 128) << height : ((i * 128) << height) + 1, :]
    for t in range(3):
        tile = jnp.transpose(coarse[t * 128 : t * 128 + 128, :])
        top_ref[t * 8 : t * 8 + 8, :] = tile[32:40]

    base = (pos - 1) * LEAVES

    def leaf(n, carry):
        own, other = carry
        count = count_ref[n]
        for s in range(16):
            source = list_ref[n * 16 + s] - base
            live = jnp.where(s < count, 1, 0)
            mine = jnp.where((source >= LEAVES) & (source < 2 * LEAVES), live, 0)
            own_ref[own] = n * 64 + source - LEAVES
            away = jnp.where(source >= LEAVES, source - LEAVES, source)
            other_ref[other] = n * 64 + away
            own += mine
            other += live - mine
        return own, other

    own, other = lax.fori_loop(0, LEAVES, leaf, (jnp.int32(0), jnp.int32(0)))
    for u in range(UNROLL):
        own_ref[own + u] = LEAVES * 64
        other_ref[other + u] = LEAVES * 64
    sizes_ref[0] = (own + UNROLL - 1) // UNROLL
    sizes_ref[1] = (other + UNROLL - 1) // UNROLL


def sort(pos, order, near_list, near_count, values, coords):
    s = jax.ShapeDtypeStruct
    return pl.pallas_call(
        sort_kernel,
        out_shape=(
            s((280, 1024), f32), s((256, 128), f32), s((24, 128), f32),
            s((640,), jnp.int32), s((640,), jnp.int32), s((2,), jnp.int32),
        ),
        in_specs=[smem] * 4 + [vmem] * 2,
        out_specs=(vmem, vmem, vmem, smem, smem, smem),
        scratch_shapes=[
            pltpu.VMEM((POINTS, 128), f32), pltpu.VMEM((POINTS, 128), f32),
            pltpu.VMEM((128, 128), f32), pltpu.VMEM((384, 128), f32),
        ],
        compiler_params=params(24),
    )(pos, order, near_list, near_count, values, coords)


def upward_kernel(packed_ref, bases_ref, transfer_ref, skel_ref, top_skel_ref, coef_ref, top_ref, coefs):
    for n in range(LEAVES):
        group, lane = n // 4, (n % 4) * 256
        values = packed_ref[group * 32 : group * 32 + 32, lane : lane + 256].astype(bf16)
        hi, lo = split(bases_ref[n])
        both = dot(jnp.concatenate([hi, lo], 0), values, NT)
        coefs[n] = both[:64] + both[64:]
    for height in range(5):
        start, up = OFFSETS[height], OFFSETS[height + 1]
        for j in range(LEAVES >> (height + 1)):
            at = start + 2 * j
            t = jnp.transpose(transfer_ref[at : at + 2].reshape(128, 64))
            hi, lo = split(coefs[at : at + 2].reshape(128, 32))
            coefs[up + j] = dot3(t, hi, lo)
    hi, lo = split(coefs[62])
    top = dot3(jnp.transpose(transfer_ref[62]), hi, lo)
    top_ref[0:16, :] = jnp.concatenate([top[q * 16 : q * 16 + 16] for q in range(4)], 1)
    for t in range(3):
        top_ref[16 + 4 * t : 16 + 4 * t + 4, :] = top_skel_ref[t * 8 : t * 8 + 4, :]
    top_ref[28:32, :] = jnp.zeros((4, 128), f32)
    coefs[63] = jnp.zeros((64, 32), f32)
    for k in range(16):
        coef_ref[k * 64 : k * 64 + 64, :] = jnp.concatenate([coefs[4 * k + q] for q in range(4)], 1)
    for k in range(32):
        coef_ref[1024 + 4 * k : 1024 + 4 * k + 4, :] = skel_ref[k * 8 : k * 8 + 4, :]


def upward(packed, bases, transfer, skel, top_skel):
    s = jax.ShapeDtypeStruct
    return pl.pallas_call(
        upward_kernel,
        out_shape=(s((1152, 128), f32), s((32, 128), f32)),
        in_specs=[vmem] * 5,
        out_specs=(vmem, vmem),
        scratch_shapes=[pltpu.VMEM((64, 64, 32), f32)],
        compiler_params=params(24),
    )(packed, bases, transfer, skel, top_skel)


def near_kernel(sources, pairs_ref, sizes_ref, own_ref, *refs):
    source_refs, refs = refs[:sources], refs[sources:]
    start_ref, refs = (refs[0], refs[1:]) if sources == 2 else (None, refs)
    out_ref, values, coords, own_rows, cols = refs
    for d in range(sources):
        for n in range(LEAVES):
            group, lane = n // 4, (n % 4) * 256
            ref = source_refs[d]
            values[d * LEAVES + n] = ref[group * 32 : group * 32 + 32, lane : lane + 256].astype(bf16)
            for c in range(3):
                at = 256 + c * 8 + group
                coords[d * LEAVES + n, c : c + 1, :] = ref[at : at + 1, lane : lane + 256]
    for n in range(LEAVES):
        group, lane = n // 4, (n % 4) * 256
        for c in range(3):
            at = 256 + c * 8 + group
            own_rows[n, c : c + 1, :] = own_ref[at : at + 1, lane : lane + 256]

    def prepare(n, carry):
        for c in range(3):
            for h in range(2):
                cols[n, c, h * 128 : h * 128 + 128, :] = column(own_rows[n, c : c + 1, h * 128 : h * 128 + 128])
        return carry

    lax.fori_loop(0, LEAVES, prepare, 0, unroll=2)
    if start_ref is None:
        out_ref[...] = jnp.zeros_like(out_ref)
    else:
        out_ref[...] = start_ref[...]

    def step(j, carry):
        for u in range(UNROLL):
            code = pairs_ref[j * UNROLL + u]
            n, m = code >> 6, code & 63
            wide = [jnp.concatenate([cols[n, c]] * 2, 1) for c in range(3)]
            hi, lo = split(matern(wide, [coords[m, c : c + 1, :] for c in range(3)]))
            v = values[m]
            out_ref[n] += dot(v, hi, NT) + dot(v, lo, NT)
        return carry

    lax.fori_loop(0, sizes_ref[sources - 1], step, 0)


def near(pairs, sizes, own, sources, start=None):
    args = [pairs, sizes, own, *sources] + ([] if start is None else [start])
    count = len(sources)
    return pl.pallas_call(
        functools.partial(near_kernel, count),
        out_shape=jax.ShapeDtypeStruct((LEAVES + 1, NVEC, LEAF), f32),
        in_specs=[smem] * 2 + [vmem] * (len(args) - 2),
        out_specs=vmem,
        scratch_shapes=[
            pltpu.VMEM((LEAVES * count, NVEC, LEAF), bf16),
            pltpu.VMEM((LEAVES * count, 8, LEAF), f32),
            pltpu.VMEM((LEAVES, 8, LEAF), f32),
            pltpu.VMEM((LEAVES + 1, 3, LEAF, 128), f32),
        ],
        compiler_params=params(40),
    )(*args)


def source_rows(left, right, live_left, live_right):
    lanes = lax.broadcasted_iota(jnp.int32, (1, 128), 1)
    live = jnp.where(lanes < 64, live_left, live_right)
    return [
        jnp.where(live > 0, jnp.where(lanes < 64, a, b), FAR_AWAY) for a, b in zip(left, right)
    ]


def couple(own_cols, slots, count, skeleton, hi_table, lo_table):
    blocks = []
    for s in range(0, 16, 2):
        rows = source_rows(
            skeleton(slots[s]), skeleton(slots[s + 1]),
            jnp.where(s < count, 1, 0), jnp.where(s + 1 < count, 1, 0),
        )
        blocks.append(matern(own_cols, rows))
    hi, lo = split(jnp.concatenate(blocks, 1))
    c_hi = jnp.concatenate([hi_table[b] for b in slots], 0)
    c_lo = jnp.concatenate([lo_table[b] for b in slots], 0)
    both = dot(jnp.concatenate([hi, lo], 0), c_hi)
    return (both[:64] + both[64:] + dot(hi, c_lo)) * 0.125


def double(row):
    lanes = lax.broadcasted_iota(jnp.int32, row.shape, 1)
    turned = pltpu.roll(row, 64, 1)
    return jnp.where(lanes < 64, row, turned), jnp.where(lanes < 64, turned, row)


def coupling_kernel(pos_ref, far_ref, count_ref, prev_ref, own_ref, next_ref, out_ref, hi_table, lo_table, skels):
    pos = pos_ref[0]
    for d, ref in enumerate((prev_ref, own_ref, next_ref)):
        for k in range(16):
            tile = ref[k * 64 : k * 64 + 64, :]
            for q in range(4):
                hi, lo = split(tile[:, q * 32 : q * 32 + 32])
                hi_table[d * 64 + 4 * k + q] = hi
                lo_table[d * 64 + 4 * k + q] = lo
        for k in range(32):
            even, odd = double(ref[1024 + 4 * k : 1024 + 4 * k + 4, :])
            skels[d * 64 + 2 * k, 0:4, :] = even
            skels[d * 64 + 2 * k + 1, 0:4, :] = odd

    def nodes(j, carry):
        for u in range(4):
            node = j * 4 + u
            used = jnp.minimum(node, NODES - 1)
            height = sum(jnp.where(used >= at, 1, 0) for at in OFFSETS[1:])
            shift = 5 - height
            offset = 64 - (64 >> height)
            first = (pos - 1) << shift
            slots = []
            for s in range(16):
                relative = far_ref[used * 16 + s] - first
                device = relative >> shift
                slots.append(device * 64 + offset + (relative - (device << shift)))
            own_cols = [column(skels[64 + used, c : c + 1, :])[0:64] for c in range(3)]
            out_ref[node] = couple(
                own_cols, slots, count_ref[used],
                lambda b: [skels[b, c : c + 1, :] for c in range(3)],
                hi_table, lo_table,
            )
        return carry

    lax.fori_loop(0, 16, nodes, 0)


def couplings(pos, far, count, prev, own, after):
    return pl.pallas_call(
        coupling_kernel,
        out_shape=jax.ShapeDtypeStruct((64, 64, 32), f32),
        in_specs=[smem] * 3 + [vmem] * 3,
        out_specs=vmem,
        scratch_shapes=[
            pltpu.VMEM((192, 64, 32), bf16), pltpu.VMEM((192, 64, 32), bf16),
            pltpu.VMEM((192, 8, 128), f32),
        ],
        compiler_params=params(32),
    )(pos, far, count, prev, own, after)


def finish_kernel(
    pos_ref, order_ref, far_ref, count_ref, gathered_ref, coarse_ref, transfer_ref, coupled_ref,
    bases_ref, near_ref, out_ref, coefs, hi_table, lo_table, skels, totals, rows, placed,
):
    pos = pos_ref[0]

    def first_level(j, carry):
        at = pl.multiple_of(j * 64, 64)
        tile = gathered_ref[pl.ds(at, 16), :] + gathered_ref[pl.ds(at + 32, 16), :]
        coefs[j] = jnp.concatenate([tile[:, q * 32 : q * 32 + 32] for q in range(4)], 0)
        return carry

    lax.fori_loop(0, 64, first_level, 0, unroll=8)
    for height in range(1, 7):
        start, total = COARSE[height], 128 >> height
        if height > 1:
            below = COARSE[height - 1]
            for j in range(total):
                at = below + 2 * j
                t = jnp.transpose(coarse_ref[at : at + 2].reshape(128, 64))
                coefs[start + j] = dot3(
                    t, hi_table[at : at + 2].reshape(128, 32), lo_table[at : at + 2].reshape(128, 32)
                )
        hi_table[start : start + total], lo_table[start : start + total] = split(coefs[start : start + total])

    device = lax.broadcasted_iota(jnp.int32, (128, 128), 1)
    node = lax.broadcasted_iota(jnp.int32, (128, 128), 0)
    for t in range(3):
        for c in range(3):
            part = gathered_ref[pl.ds(16 + 4 * t + c, 128, stride=32), :]
            for half in range(2):
                height = 2 * t + half + 1
                member = jnp.where((device >> height) == node, 1.0, 0.0).astype(f32)
                summed = lax.dot_general(
                    member[0 : max(8, 128 >> height)], part, NN,
                    precision=lax.Precision.HIGHEST, preferred_element_type=f32,
                )
                skels[height * 3 + c, 0 : max(8, 128 >> height), :] = double(summed)[half]

    above = jnp.zeros((64, 32), f32)
    for height in range(6, 0, -1):
        start = COARSE[height]
        mine = pos >> height
        slots = [far_ref[(start + mine) * 16 + s] for s in range(16)]
        own_cols = [column(skels[height * 3 + c, pl.ds(mine, 1), :])[0:64] for c in range(3)]
        coupled = couple(
            own_cols, [start + b for b in slots], count_ref[start + mine],
            lambda b: [skels[height * 3 + c, pl.ds(b - start, 1), :] for c in range(3)],
            hi_table, lo_table,
        )
        above = coupled + dot3(coarse_ref[start + mine], *split(above))

    totals[62] = coupled_ref[62] + dot3(transfer_ref[62], *split(above))
    for height in range(4, -1, -1):
        start, up = OFFSETS[height], OFFSETS[height + 1]
        for j in range(LEAVES >> (height + 1)):
            at = start + 2 * j
            lowered = dot3(transfer_ref[at : at + 2].reshape(128, 64), *split(totals[up + j]))
            totals[at : at + 2] = coupled_ref[at : at + 2] + lowered.reshape(2, 64, 32)

    def leaf(n, carry):
        total_hi, total_lo = split(jnp.transpose(totals[n]))
        base_hi, base_lo = split(bases_ref[n])
        both = dot(jnp.concatenate([total_hi, total_lo], 0), base_hi)
        far = both[:32] + both[32:] + dot(total_hi, base_lo)
        result = near_ref[n] * 0.0625 + far
        for h in range(2):
            at = pl.multiple_of(n * 256 + h * 128, 128)
            rows[pl.ds(at, 128), 0:32] = jnp.transpose(result[:, h * 128 : h * 128 + 128])
        return carry

    lax.fori_loop(0, LEAVES, leaf, 0, unroll=4)

    def scatter(step, carry):
        at = step * 32
        for u in range(32):
            placed[pl.ds(order_ref[at + u], 1), :] = rows[pl.ds(at + u, 1), :]
        return carry

    lax.fori_loop(0, POINTS // 32, scatter, 0)

    def leave(block, carry):
        at = pl.multiple_of(block * 128, 128)
        out_ref[:, pl.ds(at, 128)] = jnp.transpose(placed[pl.ds(at, 128), :])[0:32]
        return carry

    lax.fori_loop(0, POINTS // 128, leave, 0, unroll=4)


def finish(pos, order, far, count, gathered, coarse, transfer, coupled, bases, near_field):
    return pl.pallas_call(
        finish_kernel,
        out_shape=jax.ShapeDtypeStruct((NVEC, POINTS), f32),
        in_specs=[smem] * 4 + [vmem] * 6,
        out_specs=vmem,
        scratch_shapes=[
            pltpu.VMEM((126, 64, 32), f32), pltpu.VMEM((126, 64, 32), bf16), pltpu.VMEM((126, 64, 32), bf16),
            pltpu.VMEM((21, 64, 128), f32), pltpu.VMEM((63, 64, 32), f32),
            pltpu.VMEM((POINTS, 128), f32), pltpu.VMEM((POINTS, 128), f32),
        ],
        compiler_params=params(48),
    )(pos, order, far, count, gathered, coarse, transfer, coupled, bases, near_field)


def body(
    point_values, point_coords, leaf_order, leaf_bases, fine_transfer, coarse_transfer,
    near_list, near_count, fine_far, fine_far_count, coarse_far, coarse_far_count,
):
    pos = lax.axis_index(axes).astype(jnp.int32).reshape(1)
    forward = [(i, i + 1) for i in range(127)]
    backward = [(i + 1, i) for i in range(127)]
    packed, skel, top_skel, own_pairs, other_pairs, sizes = sort(
        pos, leaf_order, near_list.reshape(-1), near_count, point_values, point_coords
    )
    prev_packed = lax.ppermute(packed, axes, forward)
    next_packed = lax.ppermute(packed, axes, backward)
    coef, top = upward(packed, leaf_bases, fine_transfer, skel, top_skel)
    gathered = lax.all_gather(top, axes, axis=0, tiled=True)
    prev_coef = lax.ppermute(coef, axes, forward)
    next_coef = lax.ppermute(coef, axes, backward)
    near_field = near(own_pairs, sizes, packed, [packed])
    near_field = near(other_pairs, sizes, packed, [prev_packed, next_packed], near_field)
    coupled = couplings(pos, fine_far.reshape(-1), fine_far_count, prev_coef, coef, next_coef)
    return finish(
        pos, leaf_order, coarse_far.reshape(-1), coarse_far_count, gathered, coarse_transfer,
        fine_transfer, coupled, leaf_bases, near_field,
    )


def solution(mesh):
    return jax.shard_map(
        body,
        mesh=mesh,
        in_specs=(
            P(None, axes), P(None, axes), P(axes), P(axes, None, None), P(axes, None, None), P(),
            P(axes, None), P(axes), P(axes, None), P(axes), P(), P(),
        ),
        out_specs=P(None, axes),
        check_vma=False,
    )
```

```python
import functools

import jax
import jax.numpy as jnp
from jax import lax
from jax.experimental import pallas as pl
from jax.experimental.pallas import tpu as pltpu
from jax.sharding import PartitionSpec as P

exponent_scale = -1.4426950408889634 / 0.2
axes = ("row", "col")
f32, bf16 = jnp.float32, jnp.bfloat16
LEAVES, NODES, RANK, LEAF, NVEC, POINTS = 32, 63, 64, 256, 32, 8192
OFFSETS = (0, 32, 48, 56, 60, 62)
COARSE = (0, 0, 64, 96, 112, 120, 124)
UNROLL = 8
TRIPS = 639
FAR_AWAY = 1e9
HALF_STEP = 2.0**-23
NT = (((1,), (1,)), ((), ()))
NN = (((1,), (0,)), ((), ()))
smem = pl.BlockSpec(memory_space=pltpu.SMEM)
vmem = pl.BlockSpec(memory_space=pltpu.VMEM)
hbm = pl.BlockSpec(memory_space=pltpu.HBM)


def params(mib):
    return pltpu.CompilerParams(vmem_limit_bytes=mib << 20)


def split(x):
    hi = x.astype(bf16)
    return hi, (x - hi.astype(f32)).astype(bf16)


def dot(a, b, dims=NN):
    return lax.dot_general(a, b, dims, preferred_element_type=f32)


def dot3(a, b_hi, b_lo):
    m = a.shape[0]
    a_hi, a_lo = split(a)
    both = dot(jnp.concatenate([a_hi, a_lo], 0), b_hi)
    return both[:m] + both[m:] + dot(a_hi, b_lo)


def matern(cols, rows):
    d2 = None
    for col, row in zip(cols, rows):
        diff = col - row
        d2 = diff * diff if d2 is None else d2 + diff * diff
    return jnp.exp2(d2 * lax.rsqrt(d2) * exponent_scale)


def on_grid(z):
    return jnp.floor(z * 4194304.0 + 0.5) * 2.0**-22


def column(row):
    return jnp.transpose(jnp.broadcast_to(row, (128, 128)))


def copies(pairs, sems):
    started = [pltpu.make_async_copy(source, target, sems.at[i]) for i, (source, target) in enumerate(pairs)]
    for copy in started:
        copy.start()
    return started


def sort_kernel(
    pos_ref, list_ref, count_ref, order_hbm, values_hbm, coords_hbm, bases_hbm, transfer_hbm,
    packed_ref, coef_ref, top_ref, own_ref, other_ref,
    order_ref, values_ref, coords_ref, bases_ref, transfer_ref, rows, placed, picked, coarse, coefs, sems,
):
    pos = pos_ref[0]
    values_in, coords_in, order_in, bases_in, transfer_in = copies(
        [
            (values_hbm, values_ref), (coords_hbm, coords_ref), (order_hbm, order_ref),
            (bases_hbm, bases_ref), (transfer_hbm, transfer_ref),
        ],
        sems,
    )
    values_in.wait()
    coords_in.wait()

    def enter(block, carry):
        at = pl.multiple_of(block * 128, 128)
        tile = jnp.concatenate(
            [
                values_ref[:, pl.ds(at, 128)].astype(f32),
                coords_ref[:, pl.ds(at, 128)],
                jnp.zeros((5, 128), f32),
            ],
            0,
        )
        rows[pl.ds(at, 128), 0:40] = jnp.transpose(tile)
        return carry

    lax.fori_loop(0, POINTS // 128, enter, 0, unroll=8)
    order_in.wait()

    def gather(step, carry):
        at = pl.multiple_of(step * 64, 64)
        here = order_ref.at[pl.ds(at, 64)]
        for u in range(64):
            placed[pl.ds(at + u, 1), :] = rows[pl.ds(here[u], 1), :]
        return carry

    lax.fori_loop(0, POINTS // 64, gather, 0)
    bases_in.wait()
    transfer_in.wait()

    base = (pos - 1) * LEAVES
    own, every = jnp.int32(0), jnp.int32(0)
    for n in range(LEAVES):
        count = count_ref[n]
        shifted = base - n * 128
        for s in range(16):
            code = list_ref[s, n] - shifted
            dead = (count - 1 - s) >> 31
            own_ref[own] = code
            other_ref[every - own] = code
            own += ((code >> 5) & 1) & ~dead
            every += 1 + dead
    other = every - own
    for u in range(UNROLL):
        own_ref[own + u] = LEAVES * 128 + LEAVES
        other_ref[other + u] = LEAVES * 128
    own_ref[TRIPS] = (own + UNROLL - 1) // UNROLL
    other_ref[TRIPS] = (other + UNROLL - 1) // UNROLL

    for block in range(POINTS // 128):
        tile = jnp.transpose(placed[block * 128 : block * 128 + 128, :])
        group, lane = block // 8, (block % 8) * 128
        packed_ref[group * 32 : group * 32 + 32, lane : lane + 128] = tile[0:32]
        for c in range(3):
            at = 256 + c * 8 + group
            packed_ref[at : at + 1, lane : lane + 128] = tile[32 + c : 33 + c]

    pair = 0
    for height in range(6):
        total = LEAVES >> height
        stride = 4 << height
        for first in range(0, total, 2):
            if total == 1:
                for i in range(64):
                    picked[i : i + 1, :] = placed[i * stride : i * stride + 1, :]
                tile = jnp.transpose(picked[...])
            else:
                tile = jnp.transpose(placed[pl.ds(first * 64 * stride, 128, stride=stride), :])
            coef_ref[1024 + 4 * pair : 1024 + 4 * pair + 4, :] = tile[32:36]
            pair += 1

    coarse[...] = jnp.zeros_like(coarse)
    for height in range(1, 7):
        share = 64 >> height
        start = (height - 1) * 64 + (pos & ((1 << height) - 1)) * share
        for i in range(share):
            coarse[pl.ds(start + i, 1), :] = placed[(i * 128) << height : ((i * 128) << height) + 1, :]
    for t in range(3):
        tile = jnp.transpose(coarse[t * 128 : t * 128 + 128, :])
        top_ref[16 + 4 * t : 16 + 4 * t + 4, :] = tile[32:36]
    top_ref[28:32, :] = jnp.zeros((4, 128), f32)

    for n in range(LEAVES):
        group, lane = n // 4, (n % 4) * 256
        values = packed_ref[group * 32 : group * 32 + 32, lane : lane + 256].astype(bf16)
        hi, lo = split(bases_ref[n])
        both = dot(jnp.concatenate([hi, lo], 0), values, NT)
        coefs[n] = both[:64] + both[64:]
    for height in range(5):
        start, up = OFFSETS[height], OFFSETS[height + 1]
        for j in range(LEAVES >> (height + 1)):
            at = start + 2 * j
            t = jnp.transpose(transfer_ref[at : at + 2].reshape(128, 64))
            hi, lo = split(coefs[at : at + 2].reshape(128, 32))
            coefs[up + j] = dot3(t, hi, lo)
    hi, lo = split(coefs[62])
    top = dot3(jnp.transpose(transfer_ref[62]), hi, lo)
    top_ref[0:16, :] = jnp.concatenate([top[q * 16 : q * 16 + 16] for q in range(4)], 1)
    coefs[63] = jnp.zeros((64, 32), f32)
    for k in range(16):
        coef_ref[k * 64 : k * 64 + 64, :] = jnp.concatenate([coefs[4 * k + q] for q in range(4)], 1)


def sort(pos, near_list, near_count, order, values, coords, bases, transfer):
    s = jax.ShapeDtypeStruct
    return pl.pallas_call(
        sort_kernel,
        out_shape=(
            s((280, 1024), f32), s((1152, 128), f32), s((32, 128), f32),
            s((640,), jnp.int32), s((640,), jnp.int32),
        ),
        in_specs=[smem] * 3 + [hbm] * 5,
        out_specs=(vmem, vmem, vmem, smem, smem),
        scratch_shapes=[
            pltpu.SMEM((POINTS,), jnp.int32), pltpu.VMEM((NVEC, POINTS), bf16), pltpu.VMEM((3, POINTS), f32),
            pltpu.VMEM((LEAVES, RANK, LEAF), f32), pltpu.VMEM((NODES, RANK, RANK), f32),
            pltpu.VMEM((POINTS, 128), f32), pltpu.VMEM((POINTS, 128), f32),
            pltpu.VMEM((128, 128), f32), pltpu.VMEM((384, 128), f32),
            pltpu.VMEM((64, 64, 32), f32), pltpu.SemaphoreType.DMA((5,)),
        ],
        compiler_params=params(60),
    )(pos, near_list, near_count, order, values, coords, bases, transfer)


def near_kernel(sources, pairs_ref, *refs):
    source_refs, refs = refs[:sources], refs[sources:]
    if sources == 2:
        start_ref, cols, out_ref, values, coords = refs
    else:
        out_ref, cols, values, coords, own_rows = refs
    for d in range(sources):
        for n in range(LEAVES):
            group, lane = n // 4, (n % 4) * 256
            ref = source_refs[d]
            values[d * LEAVES + n] = ref[group * 32 : group * 32 + 32, lane : lane + 256].astype(bf16)
            for c in range(3):
                at = 256 + c * 8 + group
                row = ref[at : at + 1, lane : lane + 256]
                coords[d * LEAVES + n, c : c + 1, :] = row if c < 2 else on_grid(row) + HALF_STEP
    if sources == 1:
        for n in range(LEAVES):
            group, lane = n // 4, (n % 4) * 256
            for c in range(3):
                at = 256 + c * 8 + group
                row = source_refs[0][at : at + 1, lane : lane + 256]
                own_rows[n, c : c + 1, :] = row if c < 2 else on_grid(row)

    def prepare(n, carry):
        for c in range(3):
            for h in range(2):
                cols[n, c, h * 128 : h * 128 + 128, :] = column(own_rows[n, c : c + 1, h * 128 : h * 128 + 128])
        return carry

    if sources == 1:
        lax.fori_loop(0, LEAVES, prepare, 0, unroll=4)
        out_ref[...] = jnp.zeros_like(out_ref)
    else:
        out_ref[...] = start_ref[...]

    def step(j, carry):
        for u in range(UNROLL):
            code = pairs_ref[j * UNROLL + u]
            n, m = code >> 7, code & 127
            m = m - LEAVES if sources == 1 else m - ((m >> 6) << 5)
            wide = [jnp.concatenate([cols[n, c]] * 2, 1) for c in range(3)]
            hi, lo = split(matern(wide, [coords[m, c : c + 1, :] for c in range(3)]))
            v = values[m]
            out_ref[n] += dot(v, hi, NT) + dot(v, lo, NT)
        return carry

    lax.fori_loop(0, pairs_ref[TRIPS], step, 0)


def near(pairs, sources, earlier=()):
    args = [pairs, *sources, *earlier]
    count = len(sources)
    result = jax.ShapeDtypeStruct((LEAVES + 1, NVEC, LEAF), f32)
    columns = jax.ShapeDtypeStruct((LEAVES + 1, 3, LEAF, 128), f32)
    scratch = [pltpu.VMEM((LEAVES * count, NVEC, LEAF), bf16), pltpu.VMEM((LEAVES * count, 8, LEAF), f32)]
    return pl.pallas_call(
        functools.partial(near_kernel, count),
        out_shape=result if earlier else (result, columns),
        in_specs=[smem] + [vmem] * (len(args) - 1),
        out_specs=vmem if earlier else (vmem, vmem),
        scratch_shapes=scratch + ([] if earlier else [pltpu.VMEM((LEAVES, 8, LEAF), f32)]),
        compiler_params=params(20),
    )(*args)


def source_rows(left, right, live_left, live_right):
    lanes = lax.broadcasted_iota(jnp.int32, (1, 128), 1)
    live = jnp.where(lanes < 64, live_left, live_right)
    rows = [jnp.where(lanes < 64, a, b) for a, b in zip(left, right)]
    return [jnp.where(live > 0, rows[0], FAR_AWAY), rows[1], rows[2] + HALF_STEP]


def couple(own_cols, slots, count, skeleton, hi_table, lo_table):
    blocks = []
    for s in range(0, 16, 2):
        rows = source_rows(
            skeleton(slots[s]), skeleton(slots[s + 1]),
            jnp.where(s < count, 1, 0), jnp.where(s + 1 < count, 1, 0),
        )
        blocks.append(matern(own_cols, rows))
    hi, lo = split(jnp.concatenate(blocks, 1))
    c_hi = jnp.concatenate([hi_table[b] for b in slots], 0)
    c_lo = jnp.concatenate([lo_table[b] for b in slots], 0)
    both = dot(jnp.concatenate([hi, lo], 0), c_hi)
    return (both[:64] + both[64:] + dot(hi, c_lo)) * 0.125


def double(row):
    lanes = lax.broadcasted_iota(jnp.int32, row.shape, 1)
    turned = pltpu.roll(row, 64, 1)
    return jnp.where(lanes < 64, row, turned), jnp.where(lanes < 64, turned, row)


def coupling_kernel(pos_ref, far_ref, count_ref, prev_ref, own_ref, next_ref, out_ref, hi_table, lo_table, skels):
    pos = pos_ref[0]
    for d, ref in enumerate((prev_ref, own_ref, next_ref)):
        for k in range(16):
            tile = ref[k * 64 : k * 64 + 64, :]
            for q in range(4):
                hi, lo = split(tile[:, q * 32 : q * 32 + 32])
                hi_table[d * 64 + 4 * k + q] = hi
                lo_table[d * 64 + 4 * k + q] = lo
        for k in range(32):
            at = 1024 + 4 * k
            even, odd = double(ref[at : at + 4, :])
            for half, tile in enumerate((even, odd)):
                skels[d * 64 + 2 * k + half, 0:2, :] = tile[0:2]
                skels[d * 64 + 2 * k + half, 2:3, :] = on_grid(tile[2:3])

    def nodes(j, carry):
        for u in range(4):
            node = j * 4 + u
            used = jnp.minimum(node, NODES - 1)
            height = sum(jnp.where(used >= at, 1, 0) for at in OFFSETS[1:])
            shift = 5 - height
            offset = 64 - (64 >> height)
            first = (pos - 1) << shift
            slots = []
            for s in range(16):
                relative = far_ref[s, used] - first
                device = relative >> shift
                slots.append(device * 64 + offset + (relative - (device << shift)))
            own_cols = [column(skels[64 + used, c : c + 1, :])[0:64] for c in range(3)]
            out_ref[node] = couple(
                own_cols, slots, count_ref[used],
                lambda b: [skels[b, c : c + 1, :] for c in range(3)],
                hi_table, lo_table,
            )
        return carry

    lax.fori_loop(0, 16, nodes, 0)


def couplings(pos, far, count, prev, own, after):
    return pl.pallas_call(
        coupling_kernel,
        out_shape=jax.ShapeDtypeStruct((64, 64, 32), f32),
        in_specs=[smem] * 3 + [vmem] * 3,
        out_specs=vmem,
        scratch_shapes=[
            pltpu.VMEM((192, 64, 32), bf16), pltpu.VMEM((192, 64, 32), bf16),
            pltpu.VMEM((192, 8, 128), f32),
        ],
        compiler_params=params(14),
    )(pos, far, count, prev, own, after)


def finish_kernel(
    pos_ref, far_ref, count_ref, order_hbm, gathered_hbm, coarse_hbm, transfer_hbm, bases_hbm,
    coupled_ref, near_ref, out_ref, order_ref, gathered_ref, coarse_ref, transfer_ref, bases_ref, coefs, hi_table, lo_table, skels, totals, rows, placed, sems,
):
    pos = pos_ref[0]
    waits = copies(
        [
            (gathered_hbm, gathered_ref), (coarse_hbm, coarse_ref), (transfer_hbm, transfer_ref),
            (bases_hbm, bases_ref), (order_hbm, order_ref),
        ],
        sems,
    )
    waits[0].wait()

    def first_level(j, carry):
        at = pl.multiple_of(j * 64, 64)
        tile = gathered_ref[pl.ds(at, 16), :] + gathered_ref[pl.ds(at + 32, 16), :]
        coefs[j] = jnp.concatenate([tile[:, q * 32 : q * 32 + 32] for q in range(4)], 0)
        return carry

    lax.fori_loop(0, 64, first_level, 0, unroll=8)

    waits[1].wait()

    def turn(s, carry):
        tile = jnp.transpose(coarse_ref[pl.ds(s, 64, stride=64), :])
        rows[pl.ds(pl.multiple_of(s * 128, 128), 126), 0:64] = tile
        return carry

    lax.fori_loop(0, 64, turn, 0, unroll=8)

    def turned(n):
        return rows[pl.ds(n, 64, stride=128), :][:, 0:64]

    for height in range(1, 7):
        start, total = COARSE[height], 128 >> height
        if height > 1:
            below = COARSE[height - 1]
            for j in range(total):
                at = below + 2 * j
                t = jnp.concatenate([turned(at), turned(at + 1)], 1)
                coefs[start + j] = dot3(
                    t, hi_table[at : at + 2].reshape(128, 32), lo_table[at : at + 2].reshape(128, 32)
                )
        hi_table[start : start + total], lo_table[start : start + total] = split(coefs[start : start + total])

    device = lax.broadcasted_iota(jnp.int32, (128, 128), 1)
    node = lax.broadcasted_iota(jnp.int32, (128, 128), 0)
    for t in range(3):
        low = 2 * t + 1
        sizes = [max(16, 128 >> low), max(16, 128 >> (low + 1))]
        member = jnp.concatenate(
            [
                jnp.where((device >> (low + half)) == node, 1.0, 0.0)[0 : sizes[half]]
                for half in range(2)
            ],
            0,
        ).astype(bf16)
        for c in range(3):
            part = gathered_ref[pl.ds(16 + 4 * t + c, 128, stride=32), :]
            hi = part.astype(bf16)
            mid, low_part = split(part - hi.astype(f32))
            summed = dot(member, hi) + dot(member, mid) + dot(member, low_part)
            summed = on_grid(summed) if c == 2 else summed
            for half in range(2):
                first = half * sizes[0]
                tile = double(summed[first : first + sizes[half]])[half]
                skels[(low + half) * 3 + c, 0 : sizes[half], :] = tile

    above = jnp.zeros((64, 32), f32)
    for height in range(6, 0, -1):
        start = COARSE[height]
        mine = pos >> height
        slots = [far_ref[s, start + mine] for s in range(16)]
        own_cols = [column(skels[height * 3 + c, pl.ds(mine, 1), :])[0:64] for c in range(3)]
        coupled = couple(
            own_cols, [start + b for b in slots], count_ref[start + mine],
            lambda b: [skels[height * 3 + c, pl.ds(b - start, 1), :] for c in range(3)],
            hi_table, lo_table,
        )
        above = coupled + dot3(jnp.transpose(turned(start + mine)), *split(above))

    waits[2].wait()
    totals[62] = coupled_ref[62] + dot3(transfer_ref[62], *split(above))
    for height in range(4, -1, -1):
        start, up = OFFSETS[height], OFFSETS[height + 1]
        for j in range(LEAVES >> (height + 1)):
            at = start + 2 * j
            lowered = dot3(transfer_ref[at : at + 2].reshape(128, 64), *split(totals[up + j]))
            totals[at : at + 2] = coupled_ref[at : at + 2] + lowered.reshape(2, 64, 32)

    def leaf(n, carry):
        total_hi, total_lo = split(jnp.transpose(totals[n]))
        base_hi, base_lo = split(bases_ref[n])
        both = dot(jnp.concatenate([total_hi, total_lo], 0), base_hi)
        far = both[:32] + both[32:] + dot(total_hi, base_lo)
        result = near_ref[n] * 0.0625 + far
        for h in range(2):
            at = pl.multiple_of(n * 256 + h * 128, 128)
            rows[pl.ds(at, 128), 0:32] = jnp.transpose(result[:, h * 128 : h * 128 + 128])
        return carry

    waits[3].wait()
    lax.fori_loop(0, LEAVES, leaf, 0, unroll=4)
    waits[4].wait()

    def scatter(step, carry):
        at = pl.multiple_of(step * 64, 64)
        here = order_ref.at[pl.ds(at, 64)]
        for u in range(64):
            placed[pl.ds(here[u], 1), :] = rows[pl.ds(at + u, 1), :]
        return carry

    lax.fori_loop(0, POINTS // 64, scatter, 0)

    def leave(block, carry):
        at = pl.multiple_of(block * 128, 128)
        out_ref[:, pl.ds(at, 128)] = jnp.transpose(placed[pl.ds(at, 128), :])[0:32]
        return carry

    lax.fori_loop(0, POINTS // 128, leave, 0, unroll=4)


def finish(pos, order, far, count, gathered, coarse, transfer, coupled, bases, near_field):
    return pl.pallas_call(
        finish_kernel,
        out_shape=jax.ShapeDtypeStruct((NVEC, POINTS), f32),
        in_specs=[smem] * 3 + [hbm] * 5 + [vmem] * 2,
        out_specs=vmem,
        scratch_shapes=[
            pltpu.SMEM((POINTS,), jnp.int32), pltpu.VMEM((4096, 128), f32), pltpu.VMEM((RANK * RANK, 126), f32),
            pltpu.VMEM((NODES, RANK, RANK), f32), pltpu.VMEM((LEAVES, RANK, LEAF), f32),
            pltpu.VMEM((126, 64, 32), f32), pltpu.VMEM((126, 64, 32), bf16), pltpu.VMEM((126, 64, 32), bf16),
            pltpu.VMEM((21, 64, 128), f32), pltpu.VMEM((63, 64, 32), f32),
            pltpu.VMEM((POINTS, 128), f32), pltpu.VMEM((POINTS, 128), f32), pltpu.SemaphoreType.DMA((5,)),
        ],
        compiler_params=params(50),
    )(pos, far, count, order, gathered, coarse, transfer, bases, coupled, near_field)


def body(
    point_values, point_coords, leaf_order, leaf_bases, fine_transfer, coarse_transfer,
    near_list, near_count, fine_far, fine_far_count, coarse_far, coarse_far_count,
):
    pos = lax.axis_index(axes).astype(jnp.int32).reshape(1)
    forward = [(i, i + 1) for i in range(127)]
    backward = [(i + 1, i) for i in range(127)]
    packed, coef, top, own_pairs, other_pairs = sort(
        pos, near_list.T, near_count, leaf_order, point_values, point_coords, leaf_bases, fine_transfer
    )
    prev_packed = lax.ppermute(packed, axes, forward)
    next_packed = lax.ppermute(packed, axes, backward)
    gathered = lax.all_gather(top, axes, axis=0, tiled=True)
    prev_coef = lax.ppermute(coef, axes, forward)
    next_coef = lax.ppermute(coef, axes, backward)
    earlier = near(own_pairs, [packed])
    near_field = near(other_pairs, [prev_packed, next_packed], earlier)
    coupled = couplings(pos, fine_far.T, fine_far_count, prev_coef, coef, next_coef)
    return finish(
        pos, leaf_order, coarse_far.T, coarse_far_count, gathered, jnp.transpose(coarse_transfer, (1, 2, 0)).reshape(RANK * RANK, 126),
        fine_transfer, coupled, leaf_bases, near_field,
    )


def solution(mesh):
    return jax.shard_map(
        body,
        mesh=mesh,
        in_specs=(
            P(None, axes), P(None, axes), P(axes), P(axes, None, None), P(axes, None, None), P(),
            P(axes, None), P(axes), P(axes, None), P(axes), P(), P(),
        ),
        out_specs=P(None, axes),
        check_vma=False,
    )
```

```python
import functools

import jax
import jax.numpy as jnp
from jax import lax
from jax.experimental import pallas as pl
from jax.experimental.pallas import tpu as pltpu
from jax.sharding import PartitionSpec as P

exponent_scale = -1.4426950408889634 / 0.2
axes = ("row", "col")
f32, bf16 = jnp.float32, jnp.bfloat16
LEAVES, NODES, RANK, LEAF, NVEC, POINTS = 32, 63, 64, 256, 32, 8192
OFFSETS = (0, 32, 48, 56, 60, 62)
COARSE = (0, 0, 64, 96, 112, 120, 124)
UNROLL, TAIL = 16, 4
TRIPS = 639
FAR_AWAY = 1e9
HALF_STEP = 2.0**-23
NT = (((1,), (1,)), ((), ()))
NN = (((1,), (0,)), ((), ()))
smem = pl.BlockSpec(memory_space=pltpu.SMEM)
vmem = pl.BlockSpec(memory_space=pltpu.VMEM)
hbm = pl.BlockSpec(memory_space=pltpu.HBM)


def params(mib):
    return pltpu.CompilerParams(vmem_limit_bytes=mib << 20)


def split(x):
    hi = x.astype(bf16)
    return hi, (x - hi.astype(f32)).astype(bf16)


def dot(a, b, dims=NN):
    return lax.dot_general(a, b, dims, preferred_element_type=f32)


def dot3(a, b_hi, b_lo):
    m = a.shape[0]
    a_hi, a_lo = split(a)
    both = dot(jnp.concatenate([a_hi, a_lo], 0), b_hi)
    return both[:m] + both[m:] + dot(a_hi, b_lo)


def matern(cols, rows):
    d2 = None
    for col, row in zip(cols, rows):
        diff = col - row
        d2 = diff * diff if d2 is None else d2 + diff * diff
    return jnp.exp2(d2 * lax.rsqrt(d2) * exponent_scale)


def on_grid(z):
    return jnp.floor(z * 4194304.0 + 0.5) * 2.0**-22


def column(row):
    return jnp.transpose(jnp.broadcast_to(row, (128, 128)))


def copies(pairs, sems):
    started = [pltpu.make_async_copy(source, target, sems.at[i]) for i, (source, target) in enumerate(pairs)]
    for copy in started:
        copy.start()
    return started


def sort_kernel(
    pos_ref, list_ref, count_ref, order_hbm, values_hbm, coords_hbm, bases_hbm, transfer_hbm,
    packed_ref, coef_ref, top_ref, own_ref, other_ref,
    order_ref, values_ref, coords_ref, bases_ref, transfer_ref, rows, placed, picked, coarse, coefs, sorted_coords, sems,
):
    pos = pos_ref[0]
    values_in, coords_in, order_in, bases_in, transfer_in = copies(
        [
            (values_hbm, values_ref), (coords_hbm, coords_ref), (order_hbm, order_ref),
            (bases_hbm, bases_ref), (transfer_hbm, transfer_ref),
        ],
        sems,
    )
    values_in.wait()
    coords_in.wait()

    def enter(block, carry):
        at = pl.multiple_of(block * 128, 128)
        tile = jnp.concatenate(
            [
                values_ref[:, pl.ds(at, 128)].astype(f32),
                coords_ref[:, pl.ds(at, 128)],
                jnp.zeros((5, 128), f32),
            ],
            0,
        )
        rows[pl.ds(at, 128), 0:40] = jnp.transpose(tile)
        return carry

    lax.fori_loop(0, POINTS // 128, enter, 0, unroll=8)
    order_in.wait()

    def leave(block):
        tile = jnp.transpose(placed[pl.ds(pl.multiple_of(block * 128, 128), 128), :])
        group, lane = block // 8, pl.multiple_of((block % 8) * 128, 128)
        packed_ref[pl.ds(pl.multiple_of(group * 32, 32), 32), pl.ds(lane, 128)] = tile[0:32]
        sorted_coords[block] = tile[32:40]

    def gather(block, carry):
        leave(jnp.maximum(block - 1, 0))
        at = pl.multiple_of(block * 128, 128)
        here = order_ref.at[pl.ds(at, 128)]
        for u in range(128):
            placed[pl.ds(at + u, 1), :] = rows[pl.ds(here[u], 1), :]
        return carry

    lax.fori_loop(0, POINTS // 128, gather, 0)
    leave(jnp.int32(POINTS // 128 - 1))
    for block in range(POINTS // 128):
        group, lane = block // 8, (block % 8) * 128
        for c in range(3):
            at = 256 + c * 8 + group
            packed_ref[at : at + 1, lane : lane + 128] = sorted_coords[block, c : c + 1, :]
    bases_in.wait()
    transfer_in.wait()

    base = (pos - 1) * LEAVES
    own, other = jnp.int32(0), jnp.int32(0)
    for n in range(LEAVES):
        shifted = base - n * 128
        codes = [list_ref[s, n] - shifted for s in range(16)]
        all_own, end = own, own + other
        for s in range(16):
            own_ref[all_own] = codes[s]
            other_ref[end + s - all_own] = codes[s]
            all_own += (codes[s] >> 5) & 1
        away = own + 16 - all_own
        own += count_ref[n] - away
        other += away
    for u in range(TAIL):
        own_ref[own + u] = LEAVES * 128 + LEAVES
        other_ref[other + u] = LEAVES * 128
    own_ref[TRIPS] = own
    other_ref[TRIPS] = other

    pair = 0
    for height in range(6):
        total = LEAVES >> height
        stride = 4 << height
        for first in range(0, total, 2):
            if total == 1:
                for i in range(64):
                    picked[i : i + 1, :] = placed[i * stride : i * stride + 1, :]
                tile = jnp.transpose(picked[...])
            else:
                tile = jnp.transpose(placed[pl.ds(first * 64 * stride, 128, stride=stride), :])
            coef_ref[1024 + 4 * pair : 1024 + 4 * pair + 4, :] = tile[32:36]
            pair += 1

    coarse[...] = jnp.zeros_like(coarse)
    for height in range(1, 7):
        share = 64 >> height
        start = (height - 1) * 64 + (pos & ((1 << height) - 1)) * share
        for i in range(share):
            coarse[pl.ds(start + i, 1), :] = placed[(i * 128) << height : ((i * 128) << height) + 1, :]
    for t in range(3):
        tile = jnp.transpose(coarse[t * 128 : t * 128 + 128, :])
        top_ref[16 + 4 * t : 16 + 4 * t + 4, :] = tile[32:36]
    top_ref[28:32, :] = jnp.zeros((4, 128), f32)

    for n in range(LEAVES):
        group, lane = n // 4, (n % 4) * 256
        values = packed_ref[group * 32 : group * 32 + 32, lane : lane + 256].astype(bf16)
        hi, lo = split(bases_ref[n])
        both = dot(jnp.concatenate([hi, lo], 0), values, NT)
        coefs[n] = both[:64] + both[64:]
    for height in range(5):
        start, up = OFFSETS[height], OFFSETS[height + 1]
        for j in range(LEAVES >> (height + 1)):
            at = start + 2 * j
            t = jnp.transpose(transfer_ref[at : at + 2].reshape(128, 64))
            hi, lo = split(coefs[at : at + 2].reshape(128, 32))
            coefs[up + j] = dot3(t, hi, lo)
    hi, lo = split(coefs[62])
    top = dot3(jnp.transpose(transfer_ref[62]), hi, lo)
    top_ref[0:16, :] = jnp.concatenate([top[q * 16 : q * 16 + 16] for q in range(4)], 1)
    coefs[63] = jnp.zeros((64, 32), f32)
    for k in range(16):
        coef_ref[k * 64 : k * 64 + 64, :] = jnp.concatenate([coefs[4 * k + q] for q in range(4)], 1)


def sort(pos, near_list, near_count, order, values, coords, bases, transfer):
    s = jax.ShapeDtypeStruct
    return pl.pallas_call(
        sort_kernel,
        out_shape=(
            s((280, 1024), f32), s((1152, 128), f32), s((32, 128), f32),
            s((640,), jnp.int32), s((640,), jnp.int32),
        ),
        in_specs=[smem] * 3 + [hbm] * 5,
        out_specs=(vmem, vmem, vmem, smem, smem),
        scratch_shapes=[
            pltpu.SMEM((POINTS,), jnp.int32), pltpu.VMEM((NVEC, POINTS), bf16), pltpu.VMEM((3, POINTS), f32),
            pltpu.VMEM((LEAVES, RANK, LEAF), f32), pltpu.VMEM((NODES, RANK, RANK), f32),
            pltpu.VMEM((POINTS, 128), f32), pltpu.VMEM((POINTS, 128), f32),
            pltpu.VMEM((128, 128), f32), pltpu.VMEM((384, 128), f32),
            pltpu.VMEM((64, 64, 32), f32), pltpu.VMEM((64, 8, 128), f32), pltpu.SemaphoreType.DMA((5,)),
        ],
        compiler_params=params(60),
    )(pos, near_list, near_count, order, values, coords, bases, transfer)


def near_kernel(sources, pairs_ref, *refs):
    source_refs, refs = refs[:sources], refs[sources:]
    if sources == 2:
        start_ref, cols, out_ref, values, coords = refs
    else:
        out_ref, cols, values, coords, own_rows = refs
    for d in range(sources):
        for n in range(LEAVES):
            group, lane = n // 4, (n % 4) * 256
            ref = source_refs[d]
            values[d * LEAVES + n] = ref[group * 32 : group * 32 + 32, lane : lane + 256].astype(bf16)
            for c in range(3):
                at = 256 + c * 8 + group
                row = ref[at : at + 1, lane : lane + 256]
                coords[d * LEAVES + n, c : c + 1, :] = row if c < 2 else on_grid(row) + HALF_STEP
    if sources == 1:
        for n in range(LEAVES):
            group, lane = n // 4, (n % 4) * 256
            for c in range(3):
                at = 256 + c * 8 + group
                row = source_refs[0][at : at + 1, lane : lane + 256]
                own_rows[n, c : c + 1, :] = row if c < 2 else on_grid(row)

    def prepare(n, carry):
        for c in range(3):
            for h in range(2):
                cols[n, c, h * 128 : h * 128 + 128, :] = column(own_rows[n, c : c + 1, h * 128 : h * 128 + 128])
        return carry

    if sources == 1:
        lax.fori_loop(0, LEAVES, prepare, 0, unroll=4)
        out_ref[...] = jnp.zeros_like(out_ref)
    else:
        out_ref[...] = start_ref[...]

    def step(width, first, j, carry):
        for u in range(width):
            code = pairs_ref[first + j * width + u]
            n, m = code >> 7, code & 127
            m = m - LEAVES if sources == 1 else m - ((m >> 6) << 5)
            wide = [jnp.concatenate([cols[n, c]] * 2, 1) for c in range(3)]
            hi, lo = split(matern(wide, [coords[m, c : c + 1, :] for c in range(3)]))
            v = values[m]
            out_ref[n] += dot(v, hi, NT) + dot(v, lo, NT)
        return carry

    live = pairs_ref[TRIPS]
    whole = live // UNROLL
    lax.fori_loop(0, whole, functools.partial(step, UNROLL, 0), 0)
    rest = live - whole * UNROLL
    lax.fori_loop(0, (rest + TAIL - 1) // TAIL, functools.partial(step, TAIL, whole * UNROLL), 0)


def near(pairs, sources, earlier=()):
    args = [pairs, *sources, *earlier]
    count = len(sources)
    result = jax.ShapeDtypeStruct((LEAVES + 1, NVEC, LEAF), f32)
    columns = jax.ShapeDtypeStruct((LEAVES + 1, 3, LEAF, 128), f32)
    scratch = [pltpu.VMEM((LEAVES * count, NVEC, LEAF), bf16), pltpu.VMEM((LEAVES * count, 8, LEAF), f32)]
    return pl.pallas_call(
        functools.partial(near_kernel, count),
        out_shape=result if earlier else (result, columns),
        in_specs=[smem] + [vmem] * (len(args) - 1),
        out_specs=vmem if earlier else (vmem, vmem),
        scratch_shapes=scratch + ([] if earlier else [pltpu.VMEM((LEAVES, 8, LEAF), f32)]),
        compiler_params=params(20),
    )(*args)


def source_rows(left, right, live_left, live_right):
    lanes = lax.broadcasted_iota(jnp.int32, (1, 128), 1)
    live = jnp.where(lanes < 64, live_left, live_right)
    rows = [jnp.where(lanes < 64, a, b) for a, b in zip(left, right)]
    return [jnp.where(live > 0, rows[0], FAR_AWAY), rows[1], rows[2] + HALF_STEP]


def couple(own_cols, slots, count, skeleton, hi_table, lo_table):
    blocks = []
    for s in range(0, len(slots), 2):
        rows = source_rows(
            skeleton(slots[s]), skeleton(slots[s + 1]),
            jnp.where(s < count, 1, 0), jnp.where(s + 1 < count, 1, 0),
        )
        blocks.append(matern(own_cols, rows))
    hi, lo = split(jnp.concatenate(blocks, 1))
    c_hi = jnp.concatenate([hi_table[b] for b in slots], 0)
    c_lo = jnp.concatenate([lo_table[b] for b in slots], 0)
    both = dot(jnp.concatenate([hi, lo], 0), c_hi)
    return (both[:64] + both[64:] + dot(hi, c_lo)) * 0.125


def double(row):
    lanes = lax.broadcasted_iota(jnp.int32, row.shape, 1)
    turned = pltpu.roll(row, 64, 1)
    return jnp.where(lanes < 64, row, turned), jnp.where(lanes < 64, turned, row)


def coupling_kernel(pos_ref, far_ref, count_ref, prev_ref, own_ref, next_ref, out_ref, hi_table, lo_table, skels, cols, work_ref):
    pos = pos_ref[0]
    for d, ref in enumerate((prev_ref, own_ref, next_ref)):
        for k in range(16):
            tile = ref[k * 64 : k * 64 + 64, :]
            for q in range(4):
                hi, lo = split(tile[:, q * 32 : q * 32 + 32])
                hi_table[d * 64 + 4 * k + q] = hi
                lo_table[d * 64 + 4 * k + q] = lo
        for k in range(32):
            at = 1024 + 4 * k
            even, odd = double(ref[at : at + 4, :])
            for half, tile in enumerate((even, odd)):
                skels[d * 64 + 2 * k + half, 0:2, :] = tile[0:2]
                skels[d * 64 + 2 * k + half, 2:3, :] = on_grid(tile[2:3])

    out_ref[...] = jnp.zeros_like(out_ref)

    def prepare(node, carry):
        for c in range(3):
            cols[node, c] = column(skels[64 + node, c : c + 1, :])[0:64]
        return carry

    lax.fori_loop(0, 64, prepare, 0, unroll=4)

    def listed(node, live):
        count = count_ref[node]
        for q in range(4):
            work_ref[live] = node * 4 + q
            live += jnp.where(4 * q < count, 1, 0)
        return live

    live = lax.fori_loop(0, NODES, listed, jnp.int32(0))
    for u in range(16):
        work_ref[live + u] = NODES * 4

    def quarters(j, carry):
        for u in range(16):
            code = work_ref[j * 16 + u]
            node, first_slot = code >> 2, (code & 3) * 4
            used = jnp.minimum(node, NODES - 1)
            height = sum(jnp.where(used >= at, 1, 0) for at in OFFSETS[1:])
            shift = 5 - height
            offset = 64 - (64 >> height)
            first = (pos - 1) << shift
            slots = []
            for s in range(4):
                relative = far_ref[first_slot + s, used] - first
                device = relative >> shift
                slots.append(device * 64 + offset + (relative - (device << shift)))
            out_ref[node] += couple(
                [cols[node, c] for c in range(3)], slots, count_ref[used] - first_slot,
                lambda b: [skels[b, c : c + 1, :] for c in range(3)],
                hi_table, lo_table,
            )
        return carry

    lax.fori_loop(0, (live + 15) // 16, quarters, 0)


def couplings(pos, far, count, prev, own, after):
    return pl.pallas_call(
        coupling_kernel,
        out_shape=jax.ShapeDtypeStruct((64, 64, 32), f32),
        in_specs=[smem] * 3 + [vmem] * 3,
        out_specs=vmem,
        scratch_shapes=[
            pltpu.VMEM((192, 64, 32), bf16), pltpu.VMEM((192, 64, 32), bf16),
            pltpu.VMEM((192, 8, 128), f32), pltpu.VMEM((64, 3, 64, 128), f32), pltpu.SMEM((272,), jnp.int32),
        ],
        compiler_params=params(20),
    )(pos, far, count, prev, own, after)


def finish_kernel(
    pos_ref, far_ref, count_ref, order_hbm, gathered_hbm, coarse_ref, transfer_ref, bases_ref,
    coupled_ref, near_ref, out_ref, order_ref, gathered_ref, coefs, hi_table, lo_table, skels, totals, rows, placed, sems,
):
    pos = pos_ref[0]
    gathered_in, order_in = copies([(gathered_hbm, gathered_ref), (order_hbm, order_ref)], sems)

    def turn(s, carry):
        tile = jnp.transpose(coarse_ref[pl.ds(s, 64, stride=64), :])
        rows[pl.ds(pl.multiple_of(s * 128, 128), 126), 0:64] = tile
        return carry

    lax.fori_loop(0, 64, turn, 0, unroll=8)

    gathered_in.wait()

    def first_level(j, carry):
        at = pl.multiple_of(j * 64, 64)
        tile = gathered_ref[pl.ds(at, 16), :] + gathered_ref[pl.ds(at + 32, 16), :]
        coefs[j] = jnp.concatenate([tile[:, q * 32 : q * 32 + 32] for q in range(4)], 0)
        return carry

    lax.fori_loop(0, 64, first_level, 0, unroll=8)

    def turned(n):
        return rows[pl.ds(n, 64, stride=128), :][:, 0:64]

    for height in range(1, 7):
        start, total = COARSE[height], 128 >> height
        if height > 1:
            below = COARSE[height - 1]
            for j in range(total):
                at = below + 2 * j
                t = jnp.concatenate([turned(at), turned(at + 1)], 1)
                coefs[start + j] = dot3(
                    t, hi_table[at : at + 2].reshape(128, 32), lo_table[at : at + 2].reshape(128, 32)
                )
        hi_table[start : start + total], lo_table[start : start + total] = split(coefs[start : start + total])

    device = lax.broadcasted_iota(jnp.int32, (128, 128), 1)
    node = lax.broadcasted_iota(jnp.int32, (128, 128), 0)
    for t in range(3):
        low = 2 * t + 1
        sizes = [max(16, 128 >> low), max(16, 128 >> (low + 1))]
        member = jnp.concatenate(
            [
                jnp.where((device >> (low + half)) == node, 1.0, 0.0)[0 : sizes[half]]
                for half in range(2)
            ],
            0,
        ).astype(bf16)
        for c in range(3):
            part = gathered_ref[pl.ds(16 + 4 * t + c, 128, stride=32), :]
            hi = part.astype(bf16)
            mid, low_part = split(part - hi.astype(f32))
            summed = dot(member, hi) + dot(member, mid) + dot(member, low_part)
            summed = on_grid(summed) if c == 2 else summed
            for half in range(2):
                first = half * sizes[0]
                tile = double(summed[first : first + sizes[half]])[half]
                skels[(low + half) * 3 + c, 0 : sizes[half], :] = tile

    above = jnp.zeros((64, 32), f32)
    for height in range(6, 0, -1):
        start = COARSE[height]
        mine = pos >> height
        slots = [far_ref[s, start + mine] for s in range(16)]
        own_cols = [column(skels[height * 3 + c, pl.ds(mine, 1), :])[0:64] for c in range(3)]
        coupled = couple(
            own_cols, [start + b for b in slots], count_ref[start + mine],
            lambda b: [skels[height * 3 + c, pl.ds(b - start, 1), :] for c in range(3)],
            hi_table, lo_table,
        )
        above = coupled + dot3(jnp.transpose(turned(start + mine)), *split(above))

    totals[62] = coupled_ref[62] + dot3(transfer_ref[62], *split(above))
    for height in range(4, -1, -1):
        start, up = OFFSETS[height], OFFSETS[height + 1]
        for j in range(LEAVES >> (height + 1)):
            at = start + 2 * j
            lowered = dot3(transfer_ref[at : at + 2].reshape(128, 64), *split(totals[up + j]))
            totals[at : at + 2] = coupled_ref[at : at + 2] + lowered.reshape(2, 64, 32)

    def leaf(n):
        total_hi, total_lo = split(jnp.transpose(totals[n]))
        base_hi, base_lo = split(bases_ref[n])
        both = dot(jnp.concatenate([total_hi, total_lo], 0), base_hi)
        far = both[:32] + both[32:] + dot(total_hi, base_lo)
        return near_ref[n] * 0.0625 + far

    def scatter(n):
        at = pl.multiple_of(n * 256, 256)
        here = order_ref.at[pl.ds(at, 256)]
        for u in range(256):
            placed[pl.ds(here[u], 1), :] = rows[pl.ds(at + u, 1), :]

    def enter(n, result):
        for h in range(2):
            at = pl.multiple_of(n * 256 + h * 128, 128)
            rows[pl.ds(at, 128), 0:32] = jnp.transpose(result[:, h * 128 : h * 128 + 128])

    def step(n, carry):
        result = leaf(n + 1)
        scatter(n)
        enter(n + 1, result)
        return carry

    order_in.wait()
    enter(0, leaf(0))
    lax.fori_loop(0, LEAVES - 1, step, 0)
    scatter(LEAVES - 1)

    def leave(block, carry):
        at = pl.multiple_of(block * 128, 128)
        out_ref[:, pl.ds(at, 128)] = jnp.transpose(placed[pl.ds(at, 128), :])[0:32]
        return carry

    lax.fori_loop(0, POINTS // 128, leave, 0, unroll=4)


def finish(pos, order, far, count, gathered, coarse, transfer, coupled, bases, near_field):
    return pl.pallas_call(
        finish_kernel,
        out_shape=jax.ShapeDtypeStruct((NVEC, POINTS), f32),
        in_specs=[smem] * 3 + [hbm] * 2 + [vmem] * 5,
        out_specs=vmem,
        scratch_shapes=[
            pltpu.SMEM((POINTS,), jnp.int32), pltpu.VMEM((4096, 128), f32),
            pltpu.VMEM((126, 64, 32), f32), pltpu.VMEM((126, 64, 32), bf16), pltpu.VMEM((126, 64, 32), bf16),
            pltpu.VMEM((21, 64, 128), f32), pltpu.VMEM((63, 64, 32), f32),
            pltpu.VMEM((POINTS, 128), f32), pltpu.VMEM((POINTS, 128), f32), pltpu.SemaphoreType.DMA((2,)),
        ],
        compiler_params=params(48),
    )(pos, far, count, order, gathered, coarse, transfer, bases, coupled, near_field)


def body(
    point_values, point_coords, leaf_order, leaf_bases, fine_transfer, coarse_transfer,
    near_list, near_count, fine_far, fine_far_count, coarse_far, coarse_far_count,
):
    pos = lax.axis_index(axes).astype(jnp.int32).reshape(1)
    forward = [(i, i + 1) for i in range(127)]
    backward = [(i + 1, i) for i in range(127)]
    packed, coef, top, own_pairs, other_pairs = sort(
        pos, near_list.T, near_count, leaf_order, point_values, point_coords, leaf_bases, fine_transfer
    )
    prev_packed = lax.ppermute(packed, axes, forward)
    next_packed = lax.ppermute(packed, axes, backward)
    gathered = lax.all_gather(top, axes, axis=0, tiled=True)
    prev_coef = lax.ppermute(coef, axes, forward)
    next_coef = lax.ppermute(coef, axes, backward)
    earlier = near(own_pairs, [packed])
    near_field = near(other_pairs, [prev_packed, next_packed], earlier)
    prev_coef, next_coef, near_field = lax.optimization_barrier((prev_coef, next_coef, near_field))
    coupled = couplings(pos, fine_far.T, fine_far_count, prev_coef, coef, next_coef)
    return finish(
        pos, leaf_order, coarse_far.T, coarse_far_count, gathered, jnp.transpose(coarse_transfer, (1, 2, 0)).reshape(RANK * RANK, 126),
        fine_transfer, coupled, leaf_bases, near_field,
    )


def solution(mesh):
    return jax.shard_map(
        body,
        mesh=mesh,
        in_specs=(
            P(None, axes), P(None, axes), P(axes), P(axes, None, None), P(axes, None, None), P(),
            P(axes, None), P(axes), P(axes, None), P(axes), P(), P(),
        ),
        out_specs=P(None, axes),
        check_vma=False,
    )
```

```python
import functools

import jax
import jax.numpy as jnp
from jax import lax
from jax.experimental import pallas as pl
from jax.experimental.pallas import tpu as pltpu
from jax.sharding import PartitionSpec as P

exponent_scale = -1.4426950408889634 / 0.2
axes = ("row", "col")
f32, bf16 = jnp.float32, jnp.bfloat16
LEAVES, NODES, RANK, LEAF, NVEC, POINTS = 32, 63, 64, 256, 32, 8192
OFFSETS = (0, 32, 48, 56, 60, 62)
COARSE = (0, 0, 64, 96, 112, 120, 124)
UNROLL, TAIL = 16, 4
TRIPS = 639
FAR_AWAY = 1e9
HALF_STEP = 2.0**-23
NT = (((1,), (1,)), ((), ()))
NN = (((1,), (0,)), ((), ()))
smem = pl.BlockSpec(memory_space=pltpu.SMEM)
vmem = pl.BlockSpec(memory_space=pltpu.VMEM)
hbm = pl.BlockSpec(memory_space=pltpu.HBM)


def params(mib):
    return pltpu.CompilerParams(vmem_limit_bytes=mib << 20)


def split(x):
    hi = x.astype(bf16)
    return hi, (x - hi.astype(f32)).astype(bf16)


def dot(a, b, dims=NN):
    return lax.dot_general(a, b, dims, preferred_element_type=f32)


def dot3(a, b_hi, b_lo):
    m = a.shape[0]
    a_hi, a_lo = split(a)
    both = dot(jnp.concatenate([a_hi, a_lo], 0), b_hi)
    return both[:m] + both[m:] + dot(a_hi, b_lo)


def matern(cols, rows):
    d2 = None
    for col, row in zip(cols, rows):
        diff = col - row
        d2 = diff * diff if d2 is None else d2 + diff * diff
    return jnp.exp2(d2 * lax.rsqrt(d2) * exponent_scale)


def on_grid(z):
    return jnp.floor(z * 4194304.0 + 0.5) * 2.0**-22


def column(row):
    return jnp.transpose(jnp.broadcast_to(row, (128, 128)))


def copies(pairs, sems):
    started = [pltpu.make_async_copy(source, target, sems.at[i]) for i, (source, target) in enumerate(pairs)]
    for copy in started:
        copy.start()
    return started


def sort_kernel(
    pos_ref, list_ref, count_ref, order_hbm, values_hbm, coords_hbm, bases_hbm, transfer_hbm,
    packed_ref, coef_ref, top_ref, own_ref, other_ref,
    order_ref, values_ref, coords_ref, bases_ref, transfer_ref, rows, placed, picked, coarse, coefs, sorted_coords, sems,
):
    pos = pos_ref[0]
    values_in, coords_in, order_in, bases_in, transfer_in = copies(
        [
            (values_hbm, values_ref), (coords_hbm, coords_ref), (order_hbm, order_ref),
            (bases_hbm, bases_ref), (transfer_hbm, transfer_ref),
        ],
        sems,
    )
    values_in.wait()
    coords_in.wait()

    def enter(block, carry):
        at = pl.multiple_of(block * 128, 128)
        tile = jnp.concatenate(
            [
                values_ref[:, pl.ds(at, 128)].astype(f32),
                coords_ref[:, pl.ds(at, 128)],
                jnp.zeros((5, 128), f32),
            ],
            0,
        )
        rows[pl.ds(at, 128), 0:40] = jnp.transpose(tile)
        return carry

    lax.fori_loop(0, POINTS // 128, enter, 0, unroll=8)
    order_in.wait()

    def leave(block):
        tile = jnp.transpose(placed[pl.ds(pl.multiple_of(block * 128, 128), 128), :])
        group, lane = block // 8, pl.multiple_of((block % 8) * 128, 128)
        packed_ref[pl.ds(pl.multiple_of(group * 32, 32), 32), pl.ds(lane, 128)] = tile[0:32]
        sorted_coords[block] = tile[32:40]

    def gather(block, carry):
        leave(jnp.maximum(block - 1, 0))
        at = pl.multiple_of(block * 128, 128)
        here = order_ref.at[pl.ds(at, 128)]
        for u in range(128):
            placed[pl.ds(at + u, 1), :] = rows[pl.ds(here[u], 1), :]
        return carry

    lax.fori_loop(0, POINTS // 128, gather, 0)
    leave(jnp.int32(POINTS // 128 - 1))
    for block in range(POINTS // 128):
        group, lane = block // 8, (block % 8) * 128
        for c in range(3):
            at = 256 + c * 8 + group
            packed_ref[at : at + 1, lane : lane + 128] = sorted_coords[block, c : c + 1, :]
    bases_in.wait()
    transfer_in.wait()

    base = (pos - 1) * LEAVES
    own, other = jnp.int32(0), jnp.int32(0)
    for n in range(LEAVES):
        shifted = base - n * 128
        codes = [list_ref[s, n] - shifted for s in range(16)]
        all_own, end = own, own + other
        for s in range(16):
            own_ref[all_own] = codes[s]
            other_ref[end + s - all_own] = codes[s]
            all_own += (codes[s] >> 5) & 1
        away = own + 16 - all_own
        own += count_ref[n] - away
        other += away
    for u in range(TAIL):
        own_ref[own + u] = LEAVES * 128 + LEAVES
        other_ref[other + u] = LEAVES * 128
    own_ref[TRIPS] = own
    other_ref[TRIPS] = other
    own_ref[TRIPS - 1] = 0
    other_ref[TRIPS - 1] = (1 - (pos & 1)) * LEAVES

    pair = 0
    for height in range(6):
        total = LEAVES >> height
        stride = 4 << height
        for first in range(0, total, 2):
            if total == 1:
                for i in range(64):
                    picked[i : i + 1, :] = placed[i * stride : i * stride + 1, :]
                tile = jnp.transpose(picked[...])
            else:
                tile = jnp.transpose(placed[pl.ds(first * 64 * stride, 128, stride=stride), :])
            coef_ref[1024 + 4 * pair : 1024 + 4 * pair + 4, :] = tile[32:36]
            pair += 1

    coarse[...] = jnp.zeros_like(coarse)
    for height in range(1, 7):
        share = 64 >> height
        start = (height - 1) * 64 + (pos & ((1 << height) - 1)) * share
        for i in range(share):
            coarse[pl.ds(start + i, 1), :] = placed[(i * 128) << height : ((i * 128) << height) + 1, :]
    for t in range(3):
        tile = jnp.transpose(coarse[t * 128 : t * 128 + 128, :])
        top_ref[16 + 4 * t : 16 + 4 * t + 4, :] = tile[32:36]
    top_ref[28:32, :] = jnp.zeros((4, 128), f32)

    for n in range(LEAVES):
        group, lane = n // 4, (n % 4) * 256
        values = packed_ref[group * 32 : group * 32 + 32, lane : lane + 256].astype(bf16)
        hi, lo = split(bases_ref[n])
        both = dot(jnp.concatenate([hi, lo], 0), values, NT)
        coefs[n] = both[:64] + both[64:]
    for height in range(5):
        start, up = OFFSETS[height], OFFSETS[height + 1]
        for j in range(LEAVES >> (height + 1)):
            at = start + 2 * j
            t = jnp.transpose(transfer_ref[at : at + 2].reshape(128, 64))
            hi, lo = split(coefs[at : at + 2].reshape(128, 32))
            coefs[up + j] = dot3(t, hi, lo)
    hi, lo = split(coefs[62])
    top = dot3(jnp.transpose(transfer_ref[62]), hi, lo)
    top_ref[0:16, :] = jnp.concatenate([top[q * 16 : q * 16 + 16] for q in range(4)], 1)
    coefs[63] = jnp.zeros((64, 32), f32)
    for k in range(16):
        coef_ref[k * 64 : k * 64 + 64, :] = jnp.concatenate([coefs[4 * k + q] for q in range(4)], 1)


def sort(pos, near_list, near_count, order, values, coords, bases, transfer):
    s = jax.ShapeDtypeStruct
    return pl.pallas_call(
        sort_kernel,
        out_shape=(
            s((280, 1024), f32), s((1152, 128), f32), s((32, 128), f32),
            s((640,), jnp.int32), s((640,), jnp.int32),
        ),
        in_specs=[smem] * 3 + [hbm] * 5,
        out_specs=(vmem, vmem, vmem, smem, smem),
        scratch_shapes=[
            pltpu.SMEM((POINTS,), jnp.int32), pltpu.VMEM((NVEC, POINTS), bf16), pltpu.VMEM((3, POINTS), f32),
            pltpu.VMEM((LEAVES, RANK, LEAF), f32), pltpu.VMEM((NODES, RANK, RANK), f32),
            pltpu.VMEM((POINTS, 128), f32), pltpu.VMEM((POINTS, 128), f32),
            pltpu.VMEM((128, 128), f32), pltpu.VMEM((384, 128), f32),
            pltpu.VMEM((64, 64, 32), f32), pltpu.VMEM((64, 8, 128), f32), pltpu.SemaphoreType.DMA((5,)),
        ],
        compiler_params=params(60),
    )(pos, near_list, near_count, order, values, coords, bases, transfer)


def near_kernel(sources, pairs_ref, *refs):
    source_refs, refs = refs[:sources], refs[sources:]
    if sources == 2:
        start_ref, cols, out_ref, values, coords = refs
    else:
        out_ref, cols, values, coords, own_rows = refs
    for d in range(sources):
        for n in range(LEAVES):
            group, lane = n // 4, (n % 4) * 256
            ref = source_refs[d]
            values[d * LEAVES + n] = ref[group * 32 : group * 32 + 32, lane : lane + 256].astype(bf16)
            for c in range(3):
                at = 256 + c * 8 + group
                row = ref[at : at + 1, lane : lane + 256]
                coords[d * LEAVES + n, c : c + 1, :] = row if c < 2 else on_grid(row) + HALF_STEP
    if sources == 1:
        for n in range(LEAVES):
            group, lane = n // 4, (n % 4) * 256
            for c in range(3):
                at = 256 + c * 8 + group
                row = source_refs[0][at : at + 1, lane : lane + 256]
                own_rows[n, c : c + 1, :] = row if c < 2 else on_grid(row)

    def prepare(n, carry):
        for c in range(3):
            for h in range(2):
                cols[n, c, h * 128 : h * 128 + 128, :] = column(own_rows[n, c : c + 1, h * 128 : h * 128 + 128])
        return carry

    if sources == 1:
        lax.fori_loop(0, LEAVES, prepare, 0, unroll=4)
        out_ref[...] = jnp.zeros_like(out_ref)
    else:
        out_ref[...] = start_ref[...]

    def step(width, first, j, carry):
        for u in range(width):
            code = pairs_ref[first + j * width + u]
            n, m = code >> 7, code & 127
            m = m - LEAVES if sources == 1 else (m - ((m >> 6) << 5)) ^ swap
            wide = [jnp.concatenate([cols[n, c]] * 2, 1) for c in range(3)]
            hi, lo = split(matern(wide, [coords[m, c : c + 1, :] for c in range(3)]))
            v = values[m]
            out_ref[n] += dot(v, hi, NT) + dot(v, lo, NT)
        return carry

    swap = pairs_ref[TRIPS - 1]
    live = pairs_ref[TRIPS]
    whole = live // UNROLL
    lax.fori_loop(0, whole, functools.partial(step, UNROLL, 0), 0)
    rest = live - whole * UNROLL
    lax.fori_loop(0, (rest + TAIL - 1) // TAIL, functools.partial(step, TAIL, whole * UNROLL), 0)


def near(pairs, sources, earlier=()):
    args = [pairs, *sources, *earlier]
    count = len(sources)
    result = jax.ShapeDtypeStruct((LEAVES + 1, NVEC, LEAF), f32)
    columns = jax.ShapeDtypeStruct((LEAVES + 1, 3, LEAF, 128), f32)
    scratch = [pltpu.VMEM((LEAVES * count, NVEC, LEAF), bf16), pltpu.VMEM((LEAVES * count, 8, LEAF), f32)]
    return pl.pallas_call(
        functools.partial(near_kernel, count),
        out_shape=result if earlier else (result, columns),
        in_specs=[smem] + [vmem] * (len(args) - 1),
        out_specs=vmem if earlier else (vmem, vmem),
        scratch_shapes=scratch + ([] if earlier else [pltpu.VMEM((LEAVES, 8, LEAF), f32)]),
        compiler_params=params(20),
    )(*args)


def source_rows(left, right, live_left, live_right):
    lanes = lax.broadcasted_iota(jnp.int32, (1, 128), 1)
    live = jnp.where(lanes < 64, live_left, live_right)
    rows = [jnp.where(lanes < 64, a, b) for a, b in zip(left, right)]
    return [jnp.where(live > 0, rows[0], FAR_AWAY), rows[1], rows[2] + HALF_STEP]


def couple(own_cols, slots, count, skeleton, hi_table, lo_table):
    blocks = []
    for s in range(0, len(slots), 2):
        rows = source_rows(
            skeleton(slots[s]), skeleton(slots[s + 1]),
            jnp.where(s < count, 1, 0), jnp.where(s + 1 < count, 1, 0),
        )
        blocks.append(matern(own_cols, rows))
    hi, lo = split(jnp.concatenate(blocks, 1))
    c_hi = jnp.concatenate([hi_table[b] for b in slots], 0)
    c_lo = jnp.concatenate([lo_table[b] for b in slots], 0)
    both = dot(jnp.concatenate([hi, lo], 0), c_hi)
    return (both[:64] + both[64:] + dot(hi, c_lo)) * 0.125


def double(row):
    lanes = lax.broadcasted_iota(jnp.int32, row.shape, 1)
    turned = pltpu.roll(row, 64, 1)
    return jnp.where(lanes < 64, row, turned), jnp.where(lanes < 64, turned, row)


def coupling_kernel(pos_ref, far_ref, count_ref, inner_ref, own_ref, outer_ref, out_ref, hi_table, lo_table, skels, cols, work_ref):
    pos = pos_ref[0]
    for d, ref in enumerate((inner_ref, own_ref, outer_ref)):
        for k in range(16):
            tile = ref[k * 64 : k * 64 + 64, :]
            for q in range(4):
                hi, lo = split(tile[:, q * 32 : q * 32 + 32])
                hi_table[d * 64 + 4 * k + q] = hi
                lo_table[d * 64 + 4 * k + q] = lo
        for k in range(32):
            at = 1024 + 4 * k
            even, odd = double(ref[at : at + 4, :])
            for half, tile in enumerate((even, odd)):
                skels[d * 64 + 2 * k + half, 0:2, :] = tile[0:2]
                skels[d * 64 + 2 * k + half, 2:3, :] = on_grid(tile[2:3])

    out_ref[...] = jnp.zeros_like(out_ref)

    def prepare(k, carry):
        for c in range(3):
            row = own_ref[pl.ds(1024 + 4 * k + c, 1), :]
            both = column(row if c < 2 else on_grid(row))
            cols[2 * k, c] = both[0:64]
            cols[2 * k + 1, c] = both[64:128]
        return carry

    lax.fori_loop(0, 32, prepare, 0, unroll=4)

    def listed(node, live):
        count = count_ref[node]
        for q in range(4):
            work_ref[live] = node * 4 + q
            live += jnp.where(4 * q < count, 1, 0)
        return live

    live = lax.fori_loop(0, NODES, listed, jnp.int32(0))
    for u in range(16):
        work_ref[live + u] = NODES * 4

    even = 1 - (pos & 1)

    def quarters(j, carry):
        for u in range(16):
            code = work_ref[j * 16 + u]
            node, first_slot = code >> 2, (code & 3) * 4
            used = jnp.minimum(node, NODES - 1)
            height = sum(jnp.where(used >= at, 1, 0) for at in OFFSETS[1:])
            shift = 5 - height
            offset = 64 - (64 >> height)
            first = (pos - 1) << shift
            slots = []
            for s in range(4):
                relative = far_ref[first_slot + s, used] - first
                device = relative >> shift
                held = jnp.where(even > 0, 2 - device, device)
                slots.append(held * 64 + offset + (relative - (device << shift)))
            out_ref[node] += couple(
                [cols[node, c] for c in range(3)], slots, count_ref[used] - first_slot,
                lambda b: [skels[b, c : c + 1, :] for c in range(3)],
                hi_table, lo_table,
            )
        return carry

    lax.fori_loop(0, (live + 15) // 16, quarters, 0)


def couplings(pos, far, count, inner, own, outer):
    return pl.pallas_call(
        coupling_kernel,
        out_shape=jax.ShapeDtypeStruct((64, 64, 32), f32),
        in_specs=[smem] * 3 + [vmem] * 3,
        out_specs=vmem,
        scratch_shapes=[
            pltpu.VMEM((192, 64, 32), bf16), pltpu.VMEM((192, 64, 32), bf16),
            pltpu.VMEM((192, 8, 128), f32), pltpu.VMEM((64, 3, 64, 128), f32), pltpu.SMEM((272,), jnp.int32),
        ],
        compiler_params=params(20),
    )(pos, far, count, inner, own, outer)


def finish_kernel(
    pos_ref, far_ref, count_ref, order_hbm, gathered_hbm, coarse_hbm, transfer_hbm, bases_hbm,
    coupled_ref, near_ref, out_ref, order_ref, gathered_ref, coarse_ref, transfer_ref, bases_ref, coefs, hi_table, lo_table, skels, totals, rows, placed, sems,
):
    pos = pos_ref[0]
    coarse_in, gathered_in, transfer_in, bases_in, order_in = copies(
        [
            (coarse_hbm, coarse_ref), (gathered_hbm, gathered_ref), (transfer_hbm, transfer_ref),
            (bases_hbm, bases_ref), (order_hbm, order_ref),
        ],
        sems,
    )
    coarse_in.wait()

    def turn(s, carry):
        tile = jnp.transpose(coarse_ref[pl.ds(s, 64, stride=64), :])
        rows[pl.ds(pl.multiple_of(s * 128, 128), 126), 0:64] = tile
        return carry

    lax.fori_loop(0, 64, turn, 0, unroll=8)

    def first_level(j, carry):
        at = pl.multiple_of(j * 64, 64)
        tile = gathered_ref[pl.ds(at, 16), :] + gathered_ref[pl.ds(at + 32, 16), :]
        coefs[j] = jnp.concatenate([tile[:, q * 32 : q * 32 + 32] for q in range(4)], 0)
        return carry

    gathered_in.wait()
    lax.fori_loop(0, 64, first_level, 0, unroll=8)

    def turned(n):
        return rows[pl.ds(n, 64, stride=128), :][:, 0:64]

    for height in range(1, 7):
        start, total = COARSE[height], 128 >> height
        if height > 1:
            below = COARSE[height - 1]
            for j in range(total):
                at = below + 2 * j
                t = jnp.concatenate([turned(at), turned(at + 1)], 1)
                coefs[start + j] = dot3(
                    t, hi_table[at : at + 2].reshape(128, 32), lo_table[at : at + 2].reshape(128, 32)
                )
        hi_table[start : start + total], lo_table[start : start + total] = split(coefs[start : start + total])

    device = lax.broadcasted_iota(jnp.int32, (128, 128), 1)
    node = lax.broadcasted_iota(jnp.int32, (128, 128), 0)
    for t in range(3):
        low = 2 * t + 1
        sizes = [max(16, 128 >> low), max(16, 128 >> (low + 1))]
        member = jnp.concatenate(
            [
                jnp.where((device >> (low + half)) == node, 1.0, 0.0)[0 : sizes[half]]
                for half in range(2)
            ],
            0,
        ).astype(bf16)
        for c in range(3):
            part = gathered_ref[pl.ds(16 + 4 * t + c, 128, stride=32), :]
            hi = part.astype(bf16)
            mid, low_part = split(part - hi.astype(f32))
            summed = dot(member, hi) + dot(member, mid) + dot(member, low_part)
            summed = on_grid(summed) if c == 2 else summed
            for half in range(2):
                first = half * sizes[0]
                tile = double(summed[first : first + sizes[half]])[half]
                skels[(low + half) * 3 + c, 0 : sizes[half], :] = tile

    above = jnp.zeros((64, 32), f32)
    for height in range(6, 0, -1):
        start = COARSE[height]
        mine = pos >> height
        slots = [far_ref[s, start + mine] for s in range(16)]
        own_cols = [column(skels[height * 3 + c, pl.ds(mine, 1), :])[0:64] for c in range(3)]
        coupled = couple(
            own_cols, [start + b for b in slots], count_ref[start + mine],
            lambda b: [skels[height * 3 + c, pl.ds(b - start, 1), :] for c in range(3)],
            hi_table, lo_table,
        )
        above = coupled + dot3(jnp.transpose(turned(start + mine)), *split(above))

    transfer_in.wait()
    totals[62] = coupled_ref[62] + dot3(transfer_ref[62], *split(above))
    for height in range(4, -1, -1):
        start, up = OFFSETS[height], OFFSETS[height + 1]
        for j in range(LEAVES >> (height + 1)):
            at = start + 2 * j
            lowered = dot3(transfer_ref[at : at + 2].reshape(128, 64), *split(totals[up + j]))
            totals[at : at + 2] = coupled_ref[at : at + 2] + lowered.reshape(2, 64, 32)

    def leaf(n):
        total_hi, total_lo = split(jnp.transpose(totals[n]))
        base_hi, base_lo = split(bases_ref[n])
        both = dot(jnp.concatenate([total_hi, total_lo], 0), base_hi)
        far = both[:32] + both[32:] + dot(total_hi, base_lo)
        return near_ref[n] * 0.0625 + far

    def scatter(n):
        at = pl.multiple_of(n * 256, 256)
        here = order_ref.at[pl.ds(at, 256)]
        for u in range(256):
            placed[pl.ds(here[u], 1), :] = rows[pl.ds(at + u, 1), :]

    def enter(n, result):
        for h in range(2):
            at = pl.multiple_of(n * 256 + h * 128, 128)
            rows[pl.ds(at, 128), 0:32] = jnp.transpose(result[:, h * 128 : h * 128 + 128])

    def step(n, carry):
        result = leaf(n + 1)
        scatter(n)
        enter(n + 1, result)
        return carry

    bases_in.wait()
    order_in.wait()
    enter(0, leaf(0))
    lax.fori_loop(0, LEAVES - 1, step, 0)
    scatter(LEAVES - 1)

    def leave(block, carry):
        at = pl.multiple_of(block * 128, 128)
        out_ref[:, pl.ds(at, 128)] = jnp.transpose(placed[pl.ds(at, 128), :])[0:32]
        return carry

    lax.fori_loop(0, POINTS // 128, leave, 0, unroll=4)


def finish(pos, order, far, count, gathered, coarse, transfer, coupled, bases, near_field):
    return pl.pallas_call(
        finish_kernel,
        out_shape=jax.ShapeDtypeStruct((NVEC, POINTS), f32),
        in_specs=[smem] * 3 + [hbm] * 5 + [vmem] * 2,
        out_specs=vmem,
        scratch_shapes=[
            pltpu.SMEM((POINTS,), jnp.int32), pltpu.VMEM((4096, 128), f32), pltpu.VMEM((RANK * RANK, 126), f32),
            pltpu.VMEM((NODES, RANK, RANK), f32), pltpu.VMEM((LEAVES, RANK, LEAF), f32),
            pltpu.VMEM((126, 64, 32), f32), pltpu.VMEM((126, 64, 32), bf16), pltpu.VMEM((126, 64, 32), bf16),
            pltpu.VMEM((21, 64, 128), f32), pltpu.VMEM((63, 64, 32), f32),
            pltpu.VMEM((POINTS, 128), f32), pltpu.VMEM((POINTS, 128), f32), pltpu.SemaphoreType.DMA((5,)),
        ],
        compiler_params=params(55),
    )(pos, far, count, order, gathered, coarse, transfer, bases, coupled, near_field)


def body(
    point_values, point_coords, leaf_order, leaf_bases, fine_transfer, coarse_transfer,
    near_list, near_count, fine_far, fine_far_count, coarse_far, coarse_far_count,
):
    pos = lax.axis_index(axes).astype(jnp.int32).reshape(1)
    inner = [(i, i ^ 1) for i in range(128)]
    outer = [(i, i + 1 if i & 1 else i - 1) for i in range(1, 127)]
    packed, coef, top, own_pairs, other_pairs = sort(
        pos, near_list.T, near_count, leaf_order, point_values, point_coords, leaf_bases, fine_transfer
    )
    inner_packed = lax.ppermute(packed, axes, inner)
    outer_packed = lax.ppermute(packed, axes, outer)
    gathered = lax.all_gather(top, axes, axis=0, tiled=True)
    inner_coef = lax.ppermute(coef, axes, inner)
    outer_coef = lax.ppermute(coef, axes, outer)
    earlier = near(own_pairs, [packed])
    near_field = near(other_pairs, [inner_packed, outer_packed], earlier)
    inner_coef, outer_coef, near_field = lax.optimization_barrier((inner_coef, outer_coef, near_field))
    coupled = couplings(pos, fine_far.T, fine_far_count, inner_coef, coef, outer_coef)
    return finish(
        pos, leaf_order, coarse_far.T, coarse_far_count, gathered, jnp.transpose(coarse_transfer, (1, 2, 0)).reshape(RANK * RANK, 126),
        fine_transfer, coupled, leaf_bases, near_field,
    )


def solution(mesh):
    return jax.shard_map(
        body,
        mesh=mesh,
        in_specs=(
            P(None, axes), P(None, axes), P(axes), P(axes, None, None), P(axes, None, None), P(),
            P(axes, None), P(axes), P(axes, None), P(axes), P(), P(),
        ),
        out_specs=P(None, axes),
        check_vma=False,
    )
```

```python
import functools

import jax
import jax.numpy as jnp
from jax import lax
from jax.experimental import pallas as pl
from jax.experimental.pallas import tpu as pltpu
from jax.sharding import PartitionSpec as P

exponent_scale = -1.4426950408889634 / 0.2
axes = ("row", "col")
f32, bf16 = jnp.float32, jnp.bfloat16
LEAVES, NODES, RANK, LEAF, NVEC, POINTS = 32, 63, 64, 256, 32, 8192
OFFSETS = (0, 32, 48, 56, 60, 62)
COARSE = (0, 0, 64, 96, 112, 120, 124)
UNROLL, TAIL = 16, 4
TRIPS = 639
FAR_AWAY = 1e9
HALF_STEP = 2.0**-23
NT = (((1,), (1,)), ((), ()))
NN = (((1,), (0,)), ((), ()))
smem = pl.BlockSpec(memory_space=pltpu.SMEM)
vmem = pl.BlockSpec(memory_space=pltpu.VMEM)
hbm = pl.BlockSpec(memory_space=pltpu.HBM)


def params(mib):
    return pltpu.CompilerParams(vmem_limit_bytes=mib << 20)


def split(x):
    hi = x.astype(bf16)
    return hi, (x - hi.astype(f32)).astype(bf16)


def dot(a, b, dims=NN):
    return lax.dot_general(a, b, dims, preferred_element_type=f32)


def dot3(a, b_hi, b_lo):
    m = a.shape[0]
    a_hi, a_lo = split(a)
    both = dot(jnp.concatenate([a_hi, a_lo], 0), b_hi)
    return both[:m] + both[m:] + dot(a_hi, b_lo)


def matern(cols, rows):
    d2 = None
    for col, row in zip(cols, rows):
        diff = col - row
        d2 = diff * diff if d2 is None else d2 + diff * diff
    return jnp.exp2(d2 * lax.rsqrt(d2) * exponent_scale)


def on_grid(z):
    return jnp.floor(z * 4194304.0 + 0.5) * 2.0**-22


def column(row):
    return jnp.transpose(jnp.broadcast_to(row, (128, 128)))


def copies(pairs, sems):
    started = [pltpu.make_async_copy(source, target, sems.at[i]) for i, (source, target) in enumerate(pairs)]
    for copy in started:
        copy.start()
    return started


def sort_kernel(
    pos_ref, list_ref, count_ref, order_hbm, values_hbm, coords_hbm, bases_hbm, transfer_hbm,
    packed_ref, coef_ref, top_ref, own_ref, other_ref,
    order_ref, values_ref, coords_ref, bases_ref, transfer_ref, rows, placed, picked, coarse, coefs, sorted_coords, sems,
):
    pos = pos_ref[0]
    values_in, coords_in, order_in, bases_in, transfer_in = copies(
        [
            (values_hbm, values_ref), (coords_hbm, coords_ref), (order_hbm, order_ref),
            (bases_hbm, bases_ref), (transfer_hbm, transfer_ref),
        ],
        sems,
    )
    values_in.wait()
    coords_in.wait()

    def enter(block, carry):
        at = pl.multiple_of(block * 128, 128)
        tile = jnp.concatenate(
            [
                values_ref[:, pl.ds(at, 128)].astype(f32),
                coords_ref[:, pl.ds(at, 128)],
                jnp.zeros((5, 128), f32),
            ],
            0,
        )
        rows[pl.ds(at, 128), 0:40] = jnp.transpose(tile)
        return carry

    lax.fori_loop(0, POINTS // 128, enter, 0, unroll=8)
    order_in.wait()

    def leave(block):
        tile = jnp.transpose(placed[pl.ds(pl.multiple_of(block * 128, 128), 128), :])
        group, lane = block // 8, pl.multiple_of((block % 8) * 128, 128)
        packed_ref[pl.ds(pl.multiple_of(group * 32, 32), 32), pl.ds(lane, 128)] = tile[0:32]
        sorted_coords[block] = tile[32:40]

    def gather(block, carry):
        leave(jnp.maximum(block - 1, 0))
        at = pl.multiple_of(block * 128, 128)
        here = order_ref.at[pl.ds(at, 128)]
        for u in range(128):
            placed[pl.ds(at + u, 1), :] = rows[pl.ds(here[u], 1), :]
        return carry

    lax.fori_loop(0, POINTS // 128, gather, 0)
    leave(jnp.int32(POINTS // 128 - 1))
    for block in range(POINTS // 128):
        group, lane = block // 8, (block % 8) * 128
        for c in range(3):
            at = 256 + c * 8 + group
            packed_ref[at : at + 1, lane : lane + 128] = sorted_coords[block, c : c + 1, :]
    bases_in.wait()
    transfer_in.wait()

    base = (pos - 1) * LEAVES
    own, other = jnp.int32(0), jnp.int32(0)
    for n in range(LEAVES):
        shifted = base - n * 128
        codes = [list_ref[s, n] - shifted for s in range(16)]
        all_own, end = own, own + other
        for s in range(16):
            own_ref[all_own] = codes[s]
            other_ref[end + s - all_own] = codes[s]
            all_own += (codes[s] >> 5) & 1
        away = own + 16 - all_own
        own += count_ref[n] - away
        other += away
    for u in range(TAIL):
        own_ref[own + u] = LEAVES * 128 + LEAVES
        other_ref[other + u] = LEAVES * 128
    own_ref[TRIPS] = own
    other_ref[TRIPS] = other
    own_ref[TRIPS - 1] = 0
    other_ref[TRIPS - 1] = (1 - (pos & 1)) * LEAVES

    pair = 0
    for height in range(6):
        total = LEAVES >> height
        stride = 4 << height
        for first in range(0, total, 2):
            if total == 1:
                for i in range(64):
                    picked[i : i + 1, :] = placed[i * stride : i * stride + 1, :]
                tile = jnp.transpose(picked[...])
            else:
                tile = jnp.transpose(placed[pl.ds(first * 64 * stride, 128, stride=stride), :])
            coef_ref[1024 + 4 * pair : 1024 + 4 * pair + 4, :] = tile[32:36]
            pair += 1

    coarse[...] = jnp.zeros_like(coarse)
    for height in range(1, 7):
        share = 64 >> height
        start = (height - 1) * 64 + (pos & ((1 << height) - 1)) * share
        for i in range(share):
            coarse[pl.ds(start + i, 1), :] = placed[(i * 128) << height : ((i * 128) << height) + 1, :]
    for t in range(3):
        tile = jnp.transpose(coarse[t * 128 : t * 128 + 128, :])
        top_ref[16 + 4 * t : 16 + 4 * t + 4, :] = tile[32:36]
    top_ref[28:32, :] = jnp.zeros((4, 128), f32)

    for n in range(LEAVES):
        group, lane = n // 4, (n % 4) * 256
        values = packed_ref[group * 32 : group * 32 + 32, lane : lane + 256].astype(bf16)
        hi, lo = split(bases_ref[n])
        both = dot(jnp.concatenate([hi, lo], 0), values, NT)
        coefs[n] = both[:64] + both[64:]
    for height in range(5):
        start, up = OFFSETS[height], OFFSETS[height + 1]
        for j in range(LEAVES >> (height + 1)):
            at = start + 2 * j
            t = jnp.transpose(transfer_ref[at : at + 2].reshape(128, 64))
            hi, lo = split(coefs[at : at + 2].reshape(128, 32))
            coefs[up + j] = dot3(t, hi, lo)
    hi, lo = split(coefs[62])
    top = dot3(jnp.transpose(transfer_ref[62]), hi, lo)
    top_ref[0:16, :] = jnp.concatenate([top[q * 16 : q * 16 + 16] for q in range(4)], 1)
    coefs[63] = jnp.zeros((64, 32), f32)
    for k in range(16):
        coef_ref[k * 64 : k * 64 + 64, :] = jnp.concatenate([coefs[4 * k + q] for q in range(4)], 1)


def sort(pos, near_list, near_count, order, values, coords, bases, transfer):
    s = jax.ShapeDtypeStruct
    return pl.pallas_call(
        sort_kernel,
        out_shape=(
            s((280, 1024), f32), s((1152, 128), f32), s((32, 128), f32),
            s((640,), jnp.int32), s((640,), jnp.int32),
        ),
        in_specs=[smem] * 3 + [hbm] * 5,
        out_specs=(vmem, vmem, vmem, smem, smem),
        scratch_shapes=[
            pltpu.SMEM((POINTS,), jnp.int32), pltpu.VMEM((NVEC, POINTS), bf16), pltpu.VMEM((3, POINTS), f32),
            pltpu.VMEM((LEAVES, RANK, LEAF), f32), pltpu.VMEM((NODES, RANK, RANK), f32),
            pltpu.VMEM((POINTS, 128), f32), pltpu.VMEM((POINTS, 128), f32),
            pltpu.VMEM((128, 128), f32), pltpu.VMEM((384, 128), f32),
            pltpu.VMEM((64, 64, 32), f32), pltpu.VMEM((64, 8, 128), f32), pltpu.SemaphoreType.DMA((5,)),
        ],
        compiler_params=params(60),
    )(pos, near_list, near_count, order, values, coords, bases, transfer)


def near_kernel(sources, pairs_ref, *refs):
    source_refs, refs = refs[:sources], refs[sources:]
    if sources == 2:
        start_ref, cols, out_ref, values, coords = refs
    else:
        out_ref, cols, values, coords, own_rows = refs
    for d in range(sources):
        for n in range(LEAVES):
            group, lane = n // 4, (n % 4) * 256
            ref = source_refs[d]
            values[d * LEAVES + n] = ref[group * 32 : group * 32 + 32, lane : lane + 256].astype(bf16)
            for c in range(3):
                at = 256 + c * 8 + group
                row = ref[at : at + 1, lane : lane + 256]
                coords[d * LEAVES + n, c : c + 1, :] = row if c < 2 else on_grid(row) + HALF_STEP
    if sources == 1:
        for n in range(LEAVES):
            group, lane = n // 4, (n % 4) * 256
            for c in range(3):
                at = 256 + c * 8 + group
                row = source_refs[0][at : at + 1, lane : lane + 256]
                own_rows[n, c : c + 1, :] = row if c < 2 else on_grid(row)

    def prepare(n, carry):
        for c in range(3):
            for h in range(2):
                cols[n, c, h * 128 : h * 128 + 128, :] = column(own_rows[n, c : c + 1, h * 128 : h * 128 + 128])
        return carry

    if sources == 1:
        lax.fori_loop(0, LEAVES, prepare, 0, unroll=4)
        out_ref[...] = jnp.zeros_like(out_ref)
    else:
        out_ref[...] = start_ref[...]

    def step(width, first, j, carry):
        for u in range(width):
            code = pairs_ref[first + j * width + u]
            n, m = code >> 7, code & 127
            m = m - LEAVES if sources == 1 else (m - ((m >> 6) << 5)) ^ swap
            wide = [jnp.concatenate([cols[n, c]] * 2, 1) for c in range(3)]
            hi, lo = split(matern(wide, [coords[m, c : c + 1, :] for c in range(3)]))
            v = values[m]
            out_ref[n] += dot(v, hi, NT) + dot(v, lo, NT)
        return carry

    swap = pairs_ref[TRIPS - 1]
    live = pairs_ref[TRIPS]
    whole = live // UNROLL
    lax.fori_loop(0, whole, functools.partial(step, UNROLL, 0), 0)
    rest = live - whole * UNROLL
    lax.fori_loop(0, (rest + TAIL - 1) // TAIL, functools.partial(step, TAIL, whole * UNROLL), 0)


def near(pairs, sources, earlier=()):
    args = [pairs, *sources, *earlier]
    count = len(sources)
    result = jax.ShapeDtypeStruct((LEAVES + 1, NVEC, LEAF), f32)
    columns = jax.ShapeDtypeStruct((LEAVES + 1, 3, LEAF, 128), f32)
    scratch = [pltpu.VMEM((LEAVES * count, NVEC, LEAF), bf16), pltpu.VMEM((LEAVES * count, 8, LEAF), f32)]
    return pl.pallas_call(
        functools.partial(near_kernel, count),
        out_shape=result if earlier else (result, columns),
        in_specs=[smem] + [vmem] * (len(args) - 1),
        out_specs=vmem if earlier else (vmem, vmem),
        scratch_shapes=scratch + ([] if earlier else [pltpu.VMEM((LEAVES, 8, LEAF), f32)]),
        compiler_params=params(20),
    )(*args)


def source_rows(left, right, live_left, live_right):
    lanes = lax.broadcasted_iota(jnp.int32, (1, 128), 1)
    live = jnp.where(lanes < 64, live_left, live_right)
    rows = [jnp.where(lanes < 64, a, b) for a, b in zip(left, right)]
    return [jnp.where(live > 0, rows[0], FAR_AWAY), rows[1], rows[2] + HALF_STEP]


def couple(own_cols, slots, count, skeleton, hi_table, lo_table):
    blocks = []
    for s in range(0, len(slots), 2):
        rows = source_rows(
            skeleton(slots[s]), skeleton(slots[s + 1]),
            jnp.where(s < count, 1, 0), jnp.where(s + 1 < count, 1, 0),
        )
        blocks.append(matern(own_cols, rows))
    hi, lo = split(jnp.concatenate(blocks, 1))
    c_hi = jnp.concatenate([hi_table[b] for b in slots], 0)
    c_lo = jnp.concatenate([lo_table[b] for b in slots], 0)
    both = dot(jnp.concatenate([hi, lo], 0), c_hi)
    return (both[:64] + both[64:] + dot(hi, c_lo)) * 0.125


def double(row):
    lanes = lax.broadcasted_iota(jnp.int32, row.shape, 1)
    turned = pltpu.roll(row, 64, 1)
    return jnp.where(lanes < 64, row, turned), jnp.where(lanes < 64, turned, row)


def coupling_kernel(pos_ref, far_ref, count_ref, inner_ref, own_ref, outer_ref, out_ref, hi_table, lo_table, skels, cols, work_ref):
    pos = pos_ref[0]
    for d, ref in enumerate((inner_ref, own_ref, outer_ref)):
        for k in range(16):
            tile = ref[k * 64 : k * 64 + 64, :]
            for q in range(4):
                hi, lo = split(tile[:, q * 32 : q * 32 + 32])
                hi_table[d * 64 + 4 * k + q] = hi
                lo_table[d * 64 + 4 * k + q] = lo
        for k in range(32):
            at = 1024 + 4 * k
            even, odd = double(ref[at : at + 4, :])
            for half, tile in enumerate((even, odd)):
                skels[d * 64 + 2 * k + half, 0:2, :] = tile[0:2]
                skels[d * 64 + 2 * k + half, 2:3, :] = on_grid(tile[2:3])

    out_ref[...] = jnp.zeros_like(out_ref)

    def prepare(k, carry):
        for c in range(3):
            row = own_ref[pl.ds(1024 + 4 * k + c, 1), :]
            both = column(row if c < 2 else on_grid(row))
            cols[2 * k, c] = both[0:64]
            cols[2 * k + 1, c] = both[64:128]
        return carry

    lax.fori_loop(0, 32, prepare, 0, unroll=4)

    def listed(node, live):
        count = count_ref[node]
        for q in range(4):
            work_ref[live] = node * 4 + q
            live += jnp.where(4 * q < count, 1, 0)
        return live

    live = lax.fori_loop(0, NODES, listed, jnp.int32(0))
    for u in range(16):
        work_ref[live + u] = NODES * 4

    even = 1 - (pos & 1)

    def quarters(j, carry):
        for u in range(16):
            code = work_ref[j * 16 + u]
            node, first_slot = code >> 2, (code & 3) * 4
            used = jnp.minimum(node, NODES - 1)
            height = sum(jnp.where(used >= at, 1, 0) for at in OFFSETS[1:])
            shift = 5 - height
            offset = 64 - (64 >> height)
            first = (pos - 1) << shift
            slots = []
            for s in range(4):
                relative = far_ref[first_slot + s, used] - first
                device = relative >> shift
                held = jnp.where(even > 0, 2 - device, device)
                slots.append(held * 64 + offset + (relative - (device << shift)))
            out_ref[node] += couple(
                [cols[node, c] for c in range(3)], slots, count_ref[used] - first_slot,
                lambda b: [skels[b, c : c + 1, :] for c in range(3)],
                hi_table, lo_table,
            )
        return carry

    lax.fori_loop(0, (live + 15) // 16, quarters, 0)


def couplings(pos, far, count, inner, own, outer):
    return pl.pallas_call(
        coupling_kernel,
        out_shape=jax.ShapeDtypeStruct((64, 64, 32), f32),
        in_specs=[smem] * 3 + [vmem] * 3,
        out_specs=vmem,
        scratch_shapes=[
            pltpu.VMEM((192, 64, 32), bf16), pltpu.VMEM((192, 64, 32), bf16),
            pltpu.VMEM((192, 8, 128), f32), pltpu.VMEM((64, 3, 64, 128), f32), pltpu.SMEM((272,), jnp.int32),
        ],
        compiler_params=params(20),
    )(pos, far, count, inner, own, outer)


def finish_kernel(
    pos_ref, far_ref, count_ref, order_hbm, gathered_hbm, coarse_hbm, transfer_hbm, bases_hbm,
    coupled_hbm, near_hbm, out_ref, order_ref, gathered_ref, coarse_ref, transfer_ref, bases_ref,
    coupled_ref, near_ref, coefs, hi_table, lo_table, skels, totals, rows, placed, sems,
):
    pos = pos_ref[0]
    coarse_in, gathered_in, transfer_in, bases_in, order_in, coupled_in, near_in = copies(
        [
            (coarse_hbm, coarse_ref), (gathered_hbm, gathered_ref), (transfer_hbm, transfer_ref),
            (bases_hbm, bases_ref), (order_hbm, order_ref), (coupled_hbm, coupled_ref), (near_hbm, near_ref),
        ],
        sems,
    )
    coarse_in.wait()

    def turn(s, carry):
        tile = jnp.transpose(coarse_ref[pl.ds(s, 64, stride=64), :])
        rows[pl.ds(pl.multiple_of(s * 128, 128), 126), 0:64] = tile
        return carry

    lax.fori_loop(0, 64, turn, 0, unroll=8)

    def first_level(j, carry):
        at = pl.multiple_of(j * 64, 64)
        tile = gathered_ref[pl.ds(at, 16), :] + gathered_ref[pl.ds(at + 32, 16), :]
        coefs[j] = jnp.concatenate([tile[:, q * 32 : q * 32 + 32] for q in range(4)], 0)
        return carry

    gathered_in.wait()
    lax.fori_loop(0, 64, first_level, 0, unroll=8)

    def turned(n):
        return rows[pl.ds(n, 64, stride=128), :][:, 0:64]

    for height in range(1, 7):
        start, total = COARSE[height], 128 >> height
        if height > 1:
            below = COARSE[height - 1]
            for j in range(total):
                at = below + 2 * j
                t = jnp.concatenate([turned(at), turned(at + 1)], 1)
                coefs[start + j] = dot3(
                    t, hi_table[at : at + 2].reshape(128, 32), lo_table[at : at + 2].reshape(128, 32)
                )
        hi_table[start : start + total], lo_table[start : start + total] = split(coefs[start : start + total])

    device = lax.broadcasted_iota(jnp.int32, (128, 128), 1)
    node = lax.broadcasted_iota(jnp.int32, (128, 128), 0)
    for t in range(3):
        low = 2 * t + 1
        sizes = [max(16, 128 >> low), max(16, 128 >> (low + 1))]
        member = jnp.concatenate(
            [
                jnp.where((device >> (low + half)) == node, 1.0, 0.0)[0 : sizes[half]]
                for half in range(2)
            ],
            0,
        ).astype(bf16)
        for c in range(3):
            part = gathered_ref[pl.ds(16 + 4 * t + c, 128, stride=32), :]
            hi = part.astype(bf16)
            mid, low_part = split(part - hi.astype(f32))
            summed = dot(member, hi) + dot(member, mid) + dot(member, low_part)
            summed = on_grid(summed) if c == 2 else summed
            for half in range(2):
                first = half * sizes[0]
                tile = double(summed[first : first + sizes[half]])[half]
                skels[(low + half) * 3 + c, 0 : sizes[half], :] = tile

    above = jnp.zeros((64, 32), f32)
    for height in range(6, 0, -1):
        start = COARSE[height]
        mine = pos >> height
        slots = [far_ref[s, start + mine] for s in range(16)]
        own_cols = [column(skels[height * 3 + c, pl.ds(mine, 1), :])[0:64] for c in range(3)]
        coupled = couple(
            own_cols, [start + b for b in slots], count_ref[start + mine],
            lambda b: [skels[height * 3 + c, pl.ds(b - start, 1), :] for c in range(3)],
            hi_table, lo_table,
        )
        above = coupled + dot3(jnp.transpose(turned(start + mine)), *split(above))

    transfer_in.wait()
    coupled_in.wait()
    totals[62] = coupled_ref[62] + dot3(transfer_ref[62], *split(above))
    for height in range(4, -1, -1):
        start, up = OFFSETS[height], OFFSETS[height + 1]
        for j in range(LEAVES >> (height + 1)):
            at = start + 2 * j
            lowered = dot3(transfer_ref[at : at + 2].reshape(128, 64), *split(totals[up + j]))
            totals[at : at + 2] = coupled_ref[at : at + 2] + lowered.reshape(2, 64, 32)

    def leaf(n):
        total_hi, total_lo = split(jnp.transpose(totals[n]))
        base_hi, base_lo = split(bases_ref[n])
        both = dot(jnp.concatenate([total_hi, total_lo], 0), base_hi)
        far = both[:32] + both[32:] + dot(total_hi, base_lo)
        return near_ref[n] * 0.0625 + far

    def scatter(n):
        at = pl.multiple_of(n * 256, 256)
        here = order_ref.at[pl.ds(at, 256)]
        for u in range(256):
            placed[pl.ds(here[u], 1), :] = rows[pl.ds(at + u, 1), :]

    def enter(n, result):
        for h in range(2):
            at = pl.multiple_of(n * 256 + h * 128, 128)
            rows[pl.ds(at, 128), 0:32] = jnp.transpose(result[:, h * 128 : h * 128 + 128])

    def step(n, carry):
        result = leaf(n + 1)
        scatter(n)
        enter(n + 1, result)
        return carry

    bases_in.wait()
    near_in.wait()
    order_in.wait()
    enter(0, leaf(0))
    lax.fori_loop(0, LEAVES - 1, step, 0)
    scatter(LEAVES - 1)

    def leave(block, carry):
        at = pl.multiple_of(block * 128, 128)
        out_ref[:, pl.ds(at, 128)] = jnp.transpose(placed[pl.ds(at, 128), :])[0:32]
        return carry

    lax.fori_loop(0, POINTS // 128, leave, 0, unroll=4)


def finish(pos, order, far, count, gathered, coarse, transfer, coupled, bases, near_field):
    return pl.pallas_call(
        finish_kernel,
        out_shape=jax.ShapeDtypeStruct((NVEC, POINTS), f32),
        in_specs=[smem] * 3 + [hbm] * 7,
        out_specs=vmem,
        scratch_shapes=[
            pltpu.SMEM((POINTS,), jnp.int32), pltpu.VMEM((4096, 128), f32), pltpu.VMEM((RANK * RANK, 126), f32),
            pltpu.VMEM((NODES, RANK, RANK), f32), pltpu.VMEM((LEAVES, RANK, LEAF), f32),
            pltpu.VMEM((64, RANK, NVEC), f32), pltpu.VMEM((LEAVES + 1, NVEC, LEAF), f32),
            pltpu.VMEM((126, 64, 32), f32), pltpu.VMEM((126, 64, 32), bf16), pltpu.VMEM((126, 64, 32), bf16),
            pltpu.VMEM((21, 64, 128), f32), pltpu.VMEM((63, 64, 32), f32),
            pltpu.VMEM((POINTS, 128), f32), pltpu.VMEM((POINTS, 128), f32), pltpu.SemaphoreType.DMA((7,)),
        ],
        compiler_params=params(55),
    )(pos, far, count, order, gathered, coarse, transfer, bases, coupled, near_field)


def body(
    point_values, point_coords, leaf_order, leaf_bases, fine_transfer, coarse_transfer,
    near_list, near_count, fine_far, fine_far_count, coarse_far, coarse_far_count,
):
    pos = lax.axis_index(axes).astype(jnp.int32).reshape(1)
    inner = [(i, i ^ 1) for i in range(128)]
    outer = [(i, i + 1 if i & 1 else i - 1) for i in range(1, 127)]
    packed, coef, top, own_pairs, other_pairs = sort(
        pos, near_list.T, near_count, leaf_order, point_values, point_coords, leaf_bases, fine_transfer
    )
    inner_packed = lax.ppermute(packed, axes, inner)
    outer_packed = lax.ppermute(packed, axes, outer)
    gathered = lax.all_gather(top, axes, axis=0, tiled=True)
    inner_coef = lax.ppermute(coef, axes, inner)
    outer_coef = lax.ppermute(coef, axes, outer)
    earlier = near(own_pairs, [packed])
    near_field = near(other_pairs, [inner_packed, outer_packed], earlier)
    inner_coef, outer_coef, near_field = lax.optimization_barrier((inner_coef, outer_coef, near_field))
    coupled = couplings(pos, fine_far.T, fine_far_count, inner_coef, coef, outer_coef)
    return finish(
        pos, leaf_order, coarse_far.T, coarse_far_count, gathered, jnp.transpose(coarse_transfer, (1, 2, 0)).reshape(RANK * RANK, 126),
        fine_transfer, coupled, leaf_bases, near_field,
    )


def solution(mesh):
    return jax.shard_map(
        body,
        mesh=mesh,
        in_specs=(
            P(None, axes), P(None, axes), P(axes), P(axes, None, None), P(axes, None, None), P(),
            P(axes, None), P(axes), P(axes, None), P(axes), P(), P(),
        ),
        out_specs=P(None, axes),
        check_vma=False,
    )
```
